32 devices in a mesh: leaf: 8 (over z, x), col: 4 (over y, core).
Axes of the slice: x: 2, y: 2, z: 4, core: 2. Of those that a mesh axis runs over, the one named last changes fastest.
Arguments:
- leaf_rhs: bfloat16 [8, 2048, 512], P('leaf', 'col'), may hold values from -6 to 6
- leaf_inverse: bfloat16 [8, 2048, 2048], P('leaf', None, 'col'), may hold values from -1 to 2, as said below
- panels: bfloat16 [8, 3, 128, 2048], P('leaf', None, None, 'col'), may hold values from -1 to 1
- pattern: int32 [8, 3], P('leaf'), may hold values 0 or 1
- offsets: int32 [8, 3], P('leaf'), may hold values from 0 to 128
- sep_inverse: float32 [8, 3, 256, 256], P('leaf'), may hold values from -2 to 2, as said below
- sep_link: float32 [8, 2, 256, 256], P('leaf'), may hold values from -1 to 1, as said below
- sep_rhs: float32 [8, 3, 256, 512], P('leaf'), may hold values from -4 to 4, as said below
Outputs:
- leaf_solution: bfloat16 [8, 2048, 512], P('leaf', 'col')
- sep_solution: float32 [8, 3, 256, 512], P('leaf', None, None, 'col')
The draws below stay inside these ranges and needn't reach their ends.
Inputs may be any that keep to these rules, and one draw needn't show every extreme that they name: `pattern`: 1 where a leaf couples to its ancestor separator of that level, else 0. A coupling block touches rows offsets to offsets + 127 of its separator. `leaf_inverse`: each block is lower triangular with diagonal entries between 0.5 and 1.5. `sep_inverse`: each block is lower triangular with diagonal entries between 0.5 and 1.5; entries [i, k] are equal for all leaves i of one level-k node, the 2^(k+1) leaves that share i // 2^(k+1). `sep_link`: entries [i, k] are equal for all leaves i that share i // 2^(k+1). `sep_rhs`: entries [i, k] are equal for all leaves i that share i // 2^(k+1).
All inputs are finite; a program needn't handle non-finite values. No bound on the sum of `pattern` on one device may be relied on, other than what follows from the above.
Results may differ from the reference program's by a relative error of at most 0.0062.
Values may be sent and summed in bfloat16 or wider, within the bound.
No kernel may reach another device: no remote copies, remote signals or barrier semaphores. Data moves between devices by JAX's collectives and lax.ppermute only.
A program may use at most 64 MiB of HBM per device.

```python
import jax
import jax.numpy as jnp
from jax import lax

LEAF = 2048
SEP = 256
PR = 128
NRHS = 512
LEVELS = 3
N_LEAF = 8


def group_copies(base):
    leaves = jnp.arange(N_LEAF)
    copies = []
    for height in range(base.shape[1]):
        first_leaf = leaves // 2 ** (height + 1) * 2 ** (height + 1)
        copies.append(jnp.take(base[:, height], first_leaf, axis=0))
    return jnp.stack(copies, axis=1)


def triangular(key, count, order, spread):
    normals = jnp.clip(jax.random.normal(key, (count, order, order), jnp.float32), -4.0, 4.0)
    row_ids = lax.broadcasted_iota(jnp.int32, (order, order), 0)
    col_ids = lax.broadcasted_iota(jnp.int32, (order, order), 1)
    lower_part = (row_ids > col_ids).astype(jnp.float32)
    identity = (row_ids == col_ids).astype(jnp.float32)
    diag_vals = jax.random.uniform(jax.random.fold_in(key, 7), (count, order, 1), jnp.float32, 0.5, 1.5)
    return normals * lower_part * (spread / order ** 0.5) + identity * diag_vals


def draw_leaf_inverse(key, part):
    keys = jax.random.split(key, N_LEAF)
    return lax.map(lambda single: triangular(single, 1, LEAF, 1.0)[0].astype(jnp.bfloat16), keys)


def draw_panels(key, part):
    normals = jnp.clip(jax.random.normal(key, (N_LEAF, LEVELS, PR, LEAF), jnp.float32), -4.0, 4.0)
    scales = 1.5 / jnp.sqrt(LEAF * 2.0 ** (jnp.arange(LEVELS).astype(jnp.float32) + 1.0))
    return (normals * scales[None, :, None, None]).astype(jnp.bfloat16)


def draw_sep_inverse(key, part):
    spread = 1.0
    base = triangular(key, N_LEAF * LEVELS, SEP, spread).reshape(N_LEAF, LEVELS, SEP, SEP)
    return group_copies(base)


def draw_sep_link(key, part):
    normals = jnp.clip(jax.random.normal(key, (N_LEAF, LEVELS - 1, SEP, SEP), jnp.float32), -4.0, 4.0)
    return group_copies(normals * (0.7 / SEP ** 0.5))


def draw_sep_rhs(key, part):
    values = jnp.clip(jax.random.normal(key, (N_LEAF, LEVELS, SEP, NRHS), jnp.float32), -4.0, 4.0)
    return group_copies(values)


def with_ends(drawn, rng, least, top_value):
    longest = drawn.shape.index(max(drawn.shape))
    spots = []
    for shift in (0, 1):
        where = [jax.random.randint(jax.random.fold_in(rng, axis), (), 0, length) for axis, length in enumerate(drawn.shape)]
        where[longest] = (where[longest] + shift) % drawn.shape[longest]
        spots.append(tuple(where))
    return drawn.at[spots[0]].set(least).at[spots[1]].set(top_value)


def steps_of(key, extent, cuts, least, top_value):
    level = 1.0
    for position, parts in cuts:
        steps = jax.random.uniform(jax.random.fold_in(jax.random.fold_in(key, 6), position), (parts,), jnp.float32, least / len(cuts), top_value / len(cuts))
        level = level * jnp.repeat(jnp.exp(steps), extent[position] // parts).reshape((-1,) + (1,) * (len(extent) - 1 - position))
    return level


def centred(own_key, shape, scale, reach, pieces=(), dtype=jnp.bfloat16):
    drawn = jax.random.normal(own_key, shape, jnp.float32) * scale
    if len(pieces) > 0:
        drawn = steps_of(own_key, shape, pieces, -0.22, 0.18) * drawn
    return jnp.clip(drawn, min=-reach, max=reach).astype(dtype)


def setup_inputs(seed: int = 0) -> dict:
    key_list = jax.random.split(jax.random.key(seed), 9)
    return {
        "leaf_rhs": centred(key_list[0], (N_LEAF, LEAF, NRHS), 1.0, 6.0, ((0, 8), (1, 4))),
        "leaf_inverse": draw_leaf_inverse(jax.random.fold_in(key_list[8], 71), 0),
        "panels": draw_panels(jax.random.fold_in(key_list[8], 71), 0),
        "pattern": with_ends((jax.random.randint(key_list[3], (N_LEAF, LEVELS), 0, 4) < 3).astype(jnp.int32), jax.random.fold_in(key_list[3], 1), 0, 1),
        "offsets": with_ends(jax.random.randint(key_list[4], (N_LEAF, LEVELS), 0, SEP - PR + 1), jax.random.fold_in(key_list[4], 1), 0, SEP - PR).astype(jnp.int32),
        "sep_inverse": draw_sep_inverse(jax.random.fold_in(key_list[8], 71), 0),
        "sep_link": draw_sep_link(jax.random.fold_in(key_list[8], 71), 0),
        "sep_rhs": draw_sep_rhs(jax.random.fold_in(key_list[8], 71), 0),
    }


def forward_leaf(members):
    inverse_blk, right_blk, panel_blk = members
    solved_blk = jnp.dot(inverse_blk, right_blk, preferred_element_type=jnp.float32).astype(jnp.bfloat16)
    partial_blk = jnp.einsum("kpr,rn->kpn", panel_blk.astype(jnp.float32), solved_blk.astype(jnp.float32))
    return solved_blk, partial_blk


def place_block(partial_blk, first_row, coupling_on):
    zeros_blk = jnp.zeros((SEP, NRHS), jnp.float32)
    return lax.dynamic_update_slice(zeros_blk, coupling_on * partial_blk, (first_row.astype(jnp.int32), jnp.int32(0)))


def slice_block(sep_blk, first_row):
    return lax.dynamic_slice(sep_blk, (first_row.astype(jnp.int32), jnp.int32(0)), (PR, NRHS))


def backward_leaf(members):
    inverse_blk, solved_blk, panel_blk, rounded_blk, first_rows, pattern_row = members
    sliced = jax.vmap(slice_block)(rounded_blk, first_rows)
    sliced = sliced * pattern_row.astype(jnp.bfloat16)[:, None, None]
    coupled = jnp.einsum("kpr,kpn->rn", panel_blk.astype(jnp.float32), sliced.astype(jnp.float32))
    reduced = (solved_blk.astype(jnp.float32) - coupled).astype(jnp.bfloat16)
    final = lax.dot_general(inverse_blk, reduced, (((0,), (0,)), ((), ())), preferred_element_type=jnp.float32)
    return final.astype(jnp.bfloat16)


def reference(leaf_rhs, leaf_inverse, panels, pattern, offsets, sep_inverse, sep_link, sep_rhs):
    highest = lax.Precision.HIGHEST
    solved, partial_value = lax.map(forward_leaf, (leaf_inverse, leaf_rhs, panels))
    coupling_on = pattern.astype(jnp.float32)
    placed = jax.vmap(jax.vmap(place_block))(partial_value, offsets, coupling_on)
    forward_sols = []
    for height in range(LEVELS):
        group_size = 2 ** (height + 1)
        update = placed[:, height].reshape(N_LEAF // group_size, group_size, SEP, NRHS).sum(axis=1)
        if height > 0:
            half_size = group_size // 2
            linked = jnp.einsum("jab,jbn->jan", sep_link[::half_size, height - 1], forward_sols[height - 1], precision=highest)
            update = update + linked.reshape(N_LEAF // group_size, 2, SEP, NRHS).sum(axis=1)
        right_nodes = sep_rhs[::group_size, height]
        forward_sols.append(jnp.einsum("jab,jbn->jan", sep_inverse[::group_size, height], right_nodes - update, precision=highest))
    backward_sols = [None] * LEVELS
    for height in reversed(range(LEVELS)):
        group_size = 2 ** (height + 1)
        residue = forward_sols[height]
        if height + 1 < LEVELS:
            parent_sol = jnp.repeat(backward_sols[height + 1], 2, axis=0)
            residue = residue - jnp.einsum("jba,jbn->jan", sep_link[::group_size, height], parent_sol, precision=highest)
        backward_sols[height] = jnp.einsum("jba,jbn->jan", sep_inverse[::group_size, height], residue, precision=highest)
    sep_solution = jnp.stack([jnp.repeat(backward_sols[height], 2 ** (height + 1), axis=0) for height in range(LEVELS)], axis=1)
    rounded = sep_solution.astype(jnp.bfloat16)
    leaf_solution = lax.map(backward_leaf, (leaf_inverse, solved, panels, rounded, offsets, pattern))
    return leaf_solution, sep_solution
```

```python
import functools

import jax
import jax.numpy as jnp
from jax import lax
from jax.experimental import pallas as pl
from jax.experimental.pallas import tpu as pltpu
from jax.sharding import PartitionSpec as P

F32 = jnp.float32
BF16 = jnp.bfloat16
HIGHEST = lax.Precision.HIGHEST
NN = (((1,), (0,)), ((), ()))
NT = (((1,), (1,)), ((), ()))
TN = (((0,), (0,)), ((), ()))
AXES = ("leaf", "col")


def moved(block, leaf_flip, col_flip):
    leaves, groups = lax.axis_size("leaf"), lax.axis_size("col")
    route = [
        (leaf * groups + col, (leaf ^ leaf_flip) * groups + (col ^ col_flip))
        for leaf in range(leaves)
        for col in range(groups)
    ]
    return lax.ppermute(block, AXES, route)


def call(body, outs, smem, vmem, scratch=(), limit=24):
    specs = [pl.BlockSpec(memory_space=pltpu.SMEM)] * len(smem)
    specs += [pl.BlockSpec(memory_space=pltpu.VMEM)] * len(vmem)
    return pl.pallas_call(
        body,
        out_shape=outs,
        in_specs=specs,
        out_specs=[pl.BlockSpec(memory_space=pltpu.VMEM)] * len(outs),
        scratch_shapes=scratch,
        compiler_params=pltpu.CompilerParams(vmem_limit_bytes=limit << 20),
        cost_estimate=pl.CostEstimate(flops=0, bytes_accessed=0, transcendentals=0),
        name=getattr(body, "func", body).__name__,
    )(*smem, *vmem)


def dot(a, b, dims):
    return lax.dot_general(a, b, dims, preferred_element_type=F32)


def split(value):
    high = value.astype(BF16)
    return high, (value - high.astype(F32)).astype(BF16)


def dot_split(value, high, low, dims):
    first, second = split(value)
    return dot(first, high, dims) + (dot(first, low, dims) + dot(second, high, dims))


def rows_at(start, size):
    return pl.ds(pl.multiple_of(start, size), size)


def prepare(ids, inverse, link, rhs, q_high, q_low, k_high, k_low, right):
    column, side = ids[0], ids[1]
    levels, share, _ = right.shape
    wide = 2 * share
    for k in range(levels):
        block = inverse[k]
        high, low = split(
            lax.dot_general(block, block, TN, precision=HIGHEST, preferred_element_type=F32)
        )
        q_high[k] = high
        q_low[k] = low
        if k + 1 < levels:
            high, low = split(
                lax.dot_general(link[k], block, NN, precision=HIGHEST, preferred_element_type=F32)
            )
            k_high[k] = high
            k_low[k] = low
        part = rhs[k, :, rows_at(column * wide, wide)].T
        right[k] = jnp.where(side == 0, part[:share], part[share:])


def leaf_products(ids, inverse, rhs, keep, turned, *sends):
    column = ids[0]
    rows = rhs.shape[0]
    half = len(sends) + 1
    turned[...] = rhs[...].T
    for j in range(half):
        for top in range(2):
            block = ((column ^ j) & (half - 1)) + top * half
            value = dot(inverse[rows_at(block * rows, rows), :], rhs[...], NN)
            if j == 0:
                keep[top] = value
            else:
                sends[j - 1][top] = value.astype(BF16)


def add_products(count, ids, keep, *refs):
    low, high, high_own = refs[count:]
    value = keep[0]
    for r in refs[:count]:
        value += r[0].astype(F32)
    low[...] = value.astype(BF16)
    value = keep[1]
    for r in refs[:count]:
        value += r[1].astype(F32)
    high[...] = value.astype(BF16)
    high_own[...] = value


def panel_products(masks, ids, inverse, *refs):
    panels, out = refs[: len(masks)], refs[-1]
    column = ids[0]
    rows = inverse.shape[1]
    total = None
    for mask, panel in zip(masks, panels):
        value = dot(panel[...], inverse[rows_at((column ^ mask) * rows, rows), :], NN)
        total = value if total is None else total + value
    out[...] = total


def partials(masks, ids, inverse, early, turned, *refs):
    panels = refs[: len(masks)]
    weight, keep, *sends = refs[len(masks) :]
    scratch = sends.pop()
    column = ids[0]
    rows = inverse.shape[1]
    total = early[...]
    for mask, panel in zip(masks, panels):
        total += dot(panel[...], inverse[rows_at((column ^ mask) * rows, rows), :], NN)
    weight[...] = total.astype(BF16)
    scratch[...] = dot(turned[...], weight[...], NT)
    half = len(sends) + 1
    wide = keep.shape[0] // 2
    for j in range(half):
        for top in range(2):
            block = ((column ^ j) & (half - 1)) + top * half
            value = scratch[rows_at(block * wide, wide), :]
            if j == 0:
                keep[top * wide : (top + 1) * wide] = value
            else:
                sends[j - 1][top * wide : (top + 1) * wide] = value.astype(BF16)


def spread(count, ids, keep, *refs):
    received = refs[:count]
    own, same, other, cross = refs[count:]
    top, side = ids[2], ids[1]
    share = own.shape[0]

    def piece(which_top, which_side):
        at = rows_at((which_top * 2 + which_side) * share, share)
        value = keep[at, :]
        for r in received:
            value += r[at, :].astype(F32)
        return value

    own[...] = piece(top, side)
    same[...] = piece(1 - top, side).astype(BF16)
    other[...] = piece(top, 1 - side).astype(BF16)
    cross[...] = piece(1 - top, 1 - side).astype(BF16)


def upward(touched, ids, spots, own, same, other, cross, right, k_high, k_low, kept, *sends):
    levels, share, sep_rows = right.shape
    mine = own[...] + same[...].astype(F32)
    theirs = other[...].astype(F32) + cross[...].astype(F32)
    blank = jnp.zeros((share, sep_rows - touched), F32)

    def placed(value, row, k):
        block = value[:, k * touched : (k + 1) * touched] * spots[row + 1, k].astype(F32)
        return pltpu.roll(jnp.concatenate([block, blank], axis=1), spots[row, k], 1)

    carried = None
    for k in range(levels):
        value = placed(mine, 0, k) + placed(theirs, 2, k)
        if k > 0:
            value += carried
        kept[k] = value
        for j in range(min(k, len(sends))):
            sends[j][k - 1 - j] = value.astype(BF16)
        if k + 1 < levels:
            rest = right[k] * (0.5**k) - value
            carried = dot_split(rest, k_high[k], k_low[k], NT)


def downward(touched, lengths, ids, spots, kept, right, q_high, q_low, k_high, k_low, *refs):
    received = refs[: len(lengths)]
    solution, passed, mine, theirs = refs[len(lengths) :]
    levels, _, sep_rows = right.shape
    parent = None
    for k in reversed(range(levels)):
        value = right[k] - kept[k]
        for length, block in zip(lengths, received):
            if length <= k:
                value -= block[k - length].astype(F32)
        answer = dot_split(value, q_high[k], q_low[k], NN)
        if parent is not None:
            answer -= dot_split(parent, k_high[k], k_low[k], NN)
        parent = answer
        solution[k] = answer
        passed[k] = answer
        rounded = answer.astype(BF16).astype(F32)
        for row, out in ((0, mine), (2, theirs)):
            shift = (sep_rows - spots[row, k]) % sep_rows
            piece = pltpu.roll(rounded, shift, 1)[:, :touched] * spots[row + 1, k].astype(F32)
            out[:, k * touched : (k + 1) * touched] = piece.astype(BF16)


def leaf_transposed(count, ids, inverse, weight, *refs):
    out, weight_turned = refs[-2:]
    blocks = refs[:-2]
    column = ids[0]
    rows = inverse.shape[1]
    half = count
    weight_turned[...] = weight[...].T
    total = None
    for j in range(half):
        for top in range(2):
            block = ((column ^ j) & (half - 1)) + top * half
            value = dot(inverse[rows_at(block * rows, rows), :], blocks[2 * j + top][...], TN)
            total = value if total is None else total + value
    out[...] = total


def finish(half, ids, base, weight_turned, *refs):
    out, gathered = refs[-2:]
    blocks = refs[:-2]
    column, side, top = ids[0], ids[1], ids[2]
    share = blocks[0].shape[0]
    for j in range(half):
        inner = (column ^ j) & (half - 1)
        for n, (flip_side, flip_top) in enumerate(((0, 0), (0, 1), (1, 0), (1, 1))):
            which_top = top ^ flip_top
            which_side = side ^ flip_side
            at = ((which_top * half + inner) * 2 + which_side) * share
            gathered[rows_at(at, share), :] = blocks[4 * j + n][...]
    out[...] = (base[...] - dot(weight_turned[...], gathered[...], NT)).astype(BF16)


def assemble(ids, mine, theirs, out):
    side = ids[1]
    for k in range(mine.shape[0]):
        first = jnp.where(side == 0, mine[k], theirs[k])
        second = jnp.where(side == 0, theirs[k], mine[k])
        out[k] = jnp.concatenate([first, second], axis=0).T


def on_device(leaf_rhs, leaf_inverse, panels, pattern, offsets, sep_inverse, sep_link, sep_rhs):
    rhs, inverse = leaf_rhs[0], leaf_inverse[0]
    rows, sources = rhs.shape
    leaves, groups = lax.axis_size("leaf"), lax.axis_size("col")
    levels = leaves.bit_length() - 1
    half = groups // 2
    touched, sep_rows = panels.shape[2], sep_inverse.shape[2]
    share = sources // groups // 2
    panel = panels[0].reshape(levels * touched, rows)
    column = lax.axis_index("col")
    side = lax.axis_index("leaf") & 1
    ids = jnp.stack([column, side, column // half]).astype(jnp.int32)

    def shape(dims, dtype=F32):
        return jax.ShapeDtypeStruct(dims, dtype)

    held = {0: panel}
    for bit in reversed(range(groups.bit_length() - 1)):
        for mask in list(held):
            held[mask | 1 << bit] = moved(held[mask], 0, 1 << bit)
    spots = jnp.concatenate([offsets, pattern], axis=0)
    spots = jnp.concatenate([spots, moved(spots, 1, 0)], axis=0)

    keep, turned, *sends = call(
        leaf_products,
        [shape((2, rows, sources)), shape((sources, rows), BF16)]
        + [shape((2, rows, sources), BF16)] * (half - 1),
        [ids],
        [inverse, rhs],
    )
    q_high, q_low, k_high, k_low, right = call(
        prepare,
        [shape((levels, sep_rows, sep_rows), BF16)] * 2
        + [shape((levels - 1, sep_rows, sep_rows), BF16)] * 2
        + [shape((levels, share, sep_rows))],
        [ids],
        [sep_inverse[0], sep_link[0], sep_rhs[0]],
    )
    received = [moved(block, 0, j + 1) for j, block in enumerate(sends)]
    low, high, high_own = call(
        functools.partial(add_products, half - 1),
        [shape((rows, sources), BF16)] * 2 + [shape((rows, sources))],
        [ids],
        [keep, *received],
    )

    near = [mask for mask in held if mask < half]
    far = [mask for mask in held if mask >= half]
    early = call(
        functools.partial(panel_products, near),
        [shape(panel.shape)],
        [ids],
        [inverse] + [held[mask] for mask in near],
    )[0]
    names = [shape(panel.shape, BF16), shape((sources // half, levels * touched))]
    names += [shape((sources // half, levels * touched), BF16)] * (half - 1)
    weight, part_keep, *part_sends = call(
        functools.partial(partials, far),
        names,
        [ids],
        [inverse, early, turned] + [held[mask] for mask in far],
        [pltpu.VMEM((sources, levels * touched), F32)],
    )
    part_received = [moved(block, 0, j + 1) for j, block in enumerate(part_sends)]
    piece = (share, levels * touched)
    own, same, other, cross = call(
        functools.partial(spread, half - 1),
        [shape(piece)] + [shape(piece, BF16)] * 3,
        [ids],
        [part_keep, *part_received],
    )
    same, other, cross = moved(same, 0, half), moved(other, 1, 0), moved(cross, 1, half)

    high, own = lax.optimization_barrier((high, own))
    solved_high = (high_own + moved(high, 0, half).astype(F32)).astype(BF16)
    solved = [low, solved_high]
    for j in range(1, half):
        solved += [moved(low, 0, j), moved(solved_high, 0, j)]
    base, weight_turned = call(
        functools.partial(leaf_transposed, half),
        [shape((rows, sources)), shape((rows, levels * touched), BF16)],
        [ids],
        [inverse, weight, *solved],
    )

    kept, *up_sends = call(
        functools.partial(upward, touched),
        [shape((levels, share, sep_rows))]
        + [shape((levels - length, share, sep_rows), BF16) for length in range(1, levels)],
        [ids, spots],
        [own, same, other, cross, right, k_high, k_low],
    )
    lengths, up_received = [], []
    for delta in range(1, leaves // 2):
        lengths.append(delta.bit_length())
        up_received.append(moved(up_sends[delta.bit_length() - 1], 2 * delta, 0))
    answer, passed, mine, theirs = call(
        functools.partial(downward, touched, lengths),
        [shape((levels, share, sep_rows))] * 2 + [shape(piece, BF16)] * 2,
        [ids, spots],
        [kept, right, q_high, q_low, k_high, k_low, *up_received],
    )

    blocks = [mine, moved(mine, 0, half), moved(theirs, 1, 0), moved(theirs, 1, half)]
    passed = moved(passed, 1, 0)
    for j in range(1, half):
        blocks += [moved(block, 0, j) for block in blocks[:4]]
    final = call(
        functools.partial(finish, half),
        [shape((rows, sources), BF16)],
        [ids],
        [base, weight_turned, *blocks],
        [pltpu.VMEM((sources, levels * touched), BF16)],
    )[0]
    solution_rows = call(
        assemble, [shape((levels, sep_rows, 2 * share))], [ids], [answer, passed]
    )[0]
    return final[None], solution_rows[None]


def solution(mesh):
    in_specs = (
        P("leaf", "col", None),
        P("leaf", None, "col"),
        P("leaf", None, None, "col"),
        P("leaf", None),
        P("leaf", None),
        P("leaf", None, None, None),
        P("leaf", None, None, None),
        P("leaf", None, None, None),
    )
    out_specs = (P("leaf", "col", None), P("leaf", None, None, "col"))
    return jax.shard_map(
        on_device, mesh=mesh, in_specs=in_specs, out_specs=out_specs, check_vma=False
    )
```

```python
import functools

import jax
import jax.numpy as jnp
from jax import lax
from jax.experimental import pallas as pl
from jax.experimental.pallas import tpu as pltpu
from jax.sharding import PartitionSpec as P

F32 = jnp.float32
BF16 = jnp.bfloat16
HIGHEST = lax.Precision.HIGHEST
NN = (((1,), (0,)), ((), ()))
NT = (((1,), (1,)), ((), ()))
TN = (((0,), (0,)), ((), ()))
AXES = ("leaf", "col")


def moved(block, leaf_flip, col_flip):
    leaves, groups = lax.axis_size("leaf"), lax.axis_size("col")
    route = [
        (leaf * groups + col, (leaf ^ leaf_flip) * groups + (col ^ col_flip))
        for leaf in range(leaves)
        for col in range(groups)
    ]
    return lax.ppermute(block, AXES, route)


def call(body, outs, smem, vmem, scratch=(), limit=24):
    specs = [pl.BlockSpec(memory_space=pltpu.SMEM)] * len(smem)
    specs += [pl.BlockSpec(memory_space=pltpu.VMEM)] * len(vmem)
    return pl.pallas_call(
        body,
        out_shape=outs,
        in_specs=specs,
        out_specs=[pl.BlockSpec(memory_space=pltpu.VMEM)] * len(outs),
        scratch_shapes=scratch,
        compiler_params=pltpu.CompilerParams(vmem_limit_bytes=limit << 20),
        cost_estimate=pl.CostEstimate(flops=5 * 10**9, bytes_accessed=0, transcendentals=0),
        name=getattr(body, "func", body).__name__,
    )(*smem, *vmem)


def dot(a, b, dims):
    return lax.dot_general(a, b, dims, preferred_element_type=F32)


def split(value):
    high = value.astype(BF16)
    return high, (value - high.astype(F32)).astype(BF16)


def dot_split(value, high, low, dims):
    first, second = split(value)
    return dot(first, high, dims) + (dot(first, low, dims) + dot(second, high, dims))


def rows_at(start, size):
    return pl.ds(pl.multiple_of(start, size), size)


def prepare(ids, inverse, link, rhs, q_high, q_low, k_high, k_low, right):
    column, side = ids[0], ids[1]
    levels, share, _ = right.shape
    wide = 2 * share
    for k in range(levels):
        block = inverse[k]
        high, low = split(
            lax.dot_general(block, block, TN, precision=HIGHEST, preferred_element_type=F32)
        )
        q_high[k] = high
        q_low[k] = low
        if k + 1 < levels:
            high, low = split(
                lax.dot_general(link[k], block, NN, precision=HIGHEST, preferred_element_type=F32)
            )
            k_high[k] = high
            k_low[k] = low
        part = rhs[k, :, rows_at(column * wide, wide)].T
        right[k] = jnp.where(side == 0, part[:share], part[share:])


def leaf_products(ids, inverse, rhs, keep, turned, *sends):
    column = ids[0]
    rows = rhs.shape[0]
    half = len(sends) + 1
    turned[...] = rhs[...].T
    for j in range(half):
        for top in range(2):
            block = ((column ^ j) & (half - 1)) + top * half
            value = dot(inverse[rows_at(block * rows, rows), :], rhs[...], NN)
            if j == 0:
                keep[top] = value
            else:
                sends[j - 1][top] = value.astype(BF16)


def add_products(count, ids, keep, *refs):
    low, high, high_own = refs[count:]
    value = keep[0]
    for r in refs[:count]:
        value += r[0].astype(F32)
    low[...] = value.astype(BF16)
    value = keep[1]
    for r in refs[:count]:
        value += r[1].astype(F32)
    high[...] = value.astype(BF16)
    high_own[...] = value


def panel_products(masks, ids, inverse, *refs):
    panels, out = refs[: len(masks)], refs[-1]
    column = ids[0]
    rows = inverse.shape[1]
    total = None
    for mask, panel in zip(masks, panels):
        value = dot(panel[...], inverse[rows_at((column ^ mask) * rows, rows), :], NN)
        total = value if total is None else total + value
    out[...] = total


def partials(masks, ids, inverse, early, turned, *refs):
    panels = refs[: len(masks)]
    weight, keep, *sends = refs[len(masks) :]
    scratch = sends.pop()
    column = ids[0]
    rows = inverse.shape[1]
    total = early[...]
    for mask, panel in zip(masks, panels):
        total += dot(panel[...], inverse[rows_at((column ^ mask) * rows, rows), :], NN)
    weight[...] = total.astype(BF16)
    scratch[...] = dot(turned[...], weight[...], NT)
    half = len(sends) + 1
    wide = keep.shape[0] // 2
    for j in range(half):
        for top in range(2):
            block = ((column ^ j) & (half - 1)) + top * half
            value = scratch[rows_at(block * wide, wide), :]
            if j == 0:
                keep[top * wide : (top + 1) * wide] = value
            else:
                sends[j - 1][top * wide : (top + 1) * wide] = value.astype(BF16)


def spread(count, ids, keep, *refs):
    received = refs[:count]
    own, same, other, cross = refs[count:]
    top, side = ids[2], ids[1]
    share = own.shape[0]

    def piece(which_top, which_side):
        at = rows_at((which_top * 2 + which_side) * share, share)
        value = keep[at, :]
        for r in received:
            value += r[at, :].astype(F32)
        return value

    own[...] = piece(top, side)
    same[...] = piece(1 - top, side).astype(BF16)
    other[...] = piece(top, 1 - side).astype(BF16)
    cross[...] = piece(1 - top, 1 - side).astype(BF16)


def upward(touched, ids, spots, own, same, other, cross, right, k_high, k_low, kept, *sends):
    levels, share, sep_rows = right.shape
    mine = own[...] + same[...].astype(F32)
    theirs = other[...].astype(F32) + cross[...].astype(F32)
    blank = jnp.zeros((share, sep_rows - touched), F32)

    def placed(value, row, k):
        block = value[:, k * touched : (k + 1) * touched] * spots[row + 1, k].astype(F32)
        return pltpu.roll(jnp.concatenate([block, blank], axis=1), spots[row, k], 1)

    carried = None
    for k in range(levels):
        value = placed(mine, 0, k) + placed(theirs, 2, k)
        if k > 0:
            value += carried
        kept[k] = value
        for j in range(min(k, len(sends))):
            sends[j][k - 1 - j] = value.astype(BF16)
        if k + 1 < levels:
            rest = right[k] * (0.5**k) - value
            carried = dot_split(rest, k_high[k], k_low[k], NT)


def downward(touched, lengths, ids, spots, kept, right, q_high, q_low, k_high, k_low, *refs):
    received = refs[: len(lengths)]
    solution, passed, mine, theirs = refs[len(lengths) :]
    levels, _, sep_rows = right.shape
    parent = None
    for k in reversed(range(levels)):
        value = right[k] - kept[k]
        for length, block in zip(lengths, received):
            if length <= k:
                value -= block[k - length].astype(F32)
        answer = dot_split(value, q_high[k], q_low[k], NN)
        if parent is not None:
            answer -= dot_split(parent, k_high[k], k_low[k], NN)
        parent = answer
        solution[k] = answer
        passed[k] = answer
        rounded = answer.astype(BF16).astype(F32)
        for row, out in ((0, mine), (2, theirs)):
            shift = (sep_rows - spots[row, k]) % sep_rows
            piece = pltpu.roll(rounded, shift, 1)[:, :touched] * spots[row + 1, k].astype(F32)
            out[:, k * touched : (k + 1) * touched] = piece.astype(BF16)


def leaf_transposed(count, ids, inverse, weight, *refs):
    out, weight_turned = refs[-2:]
    blocks = refs[:-2]
    column = ids[0]
    rows = inverse.shape[1]
    half = count
    weight_turned[...] = weight[...].T
    total = None
    for j in range(half):
        for top in range(2):
            block = ((column ^ j) & (half - 1)) + top * half
            value = dot(inverse[rows_at(block * rows, rows), :], blocks[2 * j + top][...], TN)
            total = value if total is None else total + value
    out[...] = total


def finish(half, ids, base, weight_turned, *refs):
    out, gathered = refs[-2:]
    blocks = refs[:-2]
    column, side, top = ids[0], ids[1], ids[2]
    share = blocks[0].shape[0]
    for j in range(half):
        inner = (column ^ j) & (half - 1)
        for n, (flip_side, flip_top) in enumerate(((0, 0), (0, 1), (1, 0), (1, 1))):
            which_top = top ^ flip_top
            which_side = side ^ flip_side
            at = ((which_top * half + inner) * 2 + which_side) * share
            gathered[rows_at(at, share), :] = blocks[4 * j + n][...]
    out[...] = (base[...] - dot(weight_turned[...], gathered[...], NT)).astype(BF16)


def assemble(ids, mine, theirs, out):
    side = ids[1]
    for k in range(mine.shape[0]):
        first = jnp.where(side == 0, mine[k], theirs[k])
        second = jnp.where(side == 0, theirs[k], mine[k])
        out[k] = jnp.concatenate([first, second], axis=0).T


def on_device(leaf_rhs, leaf_inverse, panels, pattern, offsets, sep_inverse, sep_link, sep_rhs):
    rhs, inverse = leaf_rhs[0], leaf_inverse[0]
    rows, sources = rhs.shape
    leaves, groups = lax.axis_size("leaf"), lax.axis_size("col")
    levels = leaves.bit_length() - 1
    half = groups // 2
    touched, sep_rows = panels.shape[2], sep_inverse.shape[2]
    share = sources // groups // 2
    panel = panels[0].reshape(levels * touched, rows)
    column = lax.axis_index("col")
    side = lax.axis_index("leaf") & 1
    ids = jnp.stack([column, side, column // half]).astype(jnp.int32)

    def shape(dims, dtype=F32):
        return jax.ShapeDtypeStruct(dims, dtype)

    held = {0: panel}
    for bit in reversed(range(groups.bit_length() - 1)):
        for mask in list(held):
            held[mask | 1 << bit] = moved(held[mask], 0, 1 << bit)
    spots = jnp.concatenate([offsets, pattern], axis=0)
    spots = jnp.concatenate([spots, moved(spots, 1, 0)], axis=0)

    keep, turned, *sends = call(
        leaf_products,
        [shape((2, rows, sources)), shape((sources, rows), BF16)]
        + [shape((2, rows, sources), BF16)] * (half - 1),
        [ids],
        [inverse, rhs],
    )
    q_high, q_low, k_high, k_low, right = call(
        prepare,
        [shape((levels, sep_rows, sep_rows), BF16)] * 2
        + [shape((levels - 1, sep_rows, sep_rows), BF16)] * 2
        + [shape((levels, share, sep_rows))],
        [ids],
        [sep_inverse[0], sep_link[0], sep_rhs[0]],
    )
    received = [moved(block, 0, j + 1) for j, block in enumerate(sends)]
    low, high, high_own = call(
        functools.partial(add_products, half - 1),
        [shape((rows, sources), BF16)] * 2 + [shape((rows, sources))],
        [ids],
        [keep, *received],
    )

    near = [mask for mask in held if mask < half]
    far = [mask for mask in held if mask >= half]
    early = call(
        functools.partial(panel_products, near),
        [shape(panel.shape)],
        [ids],
        [inverse] + [held[mask] for mask in near],
    )[0]
    names = [shape(panel.shape, BF16), shape((sources // half, levels * touched))]
    names += [shape((sources // half, levels * touched), BF16)] * (half - 1)
    weight, part_keep, *part_sends = call(
        functools.partial(partials, far),
        names,
        [ids],
        [inverse, early, turned] + [held[mask] for mask in far],
        [pltpu.VMEM((sources, levels * touched), F32)],
    )
    part_received = [moved(block, 0, j + 1) for j, block in enumerate(part_sends)]
    piece = (share, levels * touched)
    own, same, other, cross = call(
        functools.partial(spread, half - 1),
        [shape(piece)] + [shape(piece, BF16)] * 3,
        [ids],
        [part_keep, *part_received],
    )
    same, other, cross = moved(same, 0, half), moved(other, 1, 0), moved(cross, 1, half)

    high, own = lax.optimization_barrier((high, own))
    solved_high = (high_own + moved(high, 0, half).astype(F32)).astype(BF16)
    solved = [low, solved_high]
    for j in range(1, half):
        solved += [moved(low, 0, j), moved(solved_high, 0, j)]
    base, weight_turned = call(
        functools.partial(leaf_transposed, half),
        [shape((rows, sources)), shape((rows, levels * touched), BF16)],
        [ids],
        [inverse, weight, *solved],
    )

    kept, *up_sends = call(
        functools.partial(upward, touched),
        [shape((levels, share, sep_rows))]
        + [shape((levels - length, share, sep_rows), BF16) for length in range(1, levels)],
        [ids, spots],
        [own, same, other, cross, right, k_high, k_low],
    )
    lengths, up_received = [], []
    for delta in range(1, leaves // 2):
        lengths.append(delta.bit_length())
        up_received.append(moved(up_sends[delta.bit_length() - 1], 2 * delta, 0))
    answer, passed, mine, theirs = call(
        functools.partial(downward, touched, lengths),
        [shape((levels, share, sep_rows))] * 2 + [shape(piece, BF16)] * 2,
        [ids, spots],
        [kept, right, q_high, q_low, k_high, k_low, *up_received],
    )

    blocks = [mine, moved(mine, 0, half), moved(theirs, 1, 0), moved(theirs, 1, half)]
    passed = moved(passed, 1, 0)
    for j in range(1, half):
        blocks += [moved(block, 0, j) for block in blocks[:4]]
    final = call(
        functools.partial(finish, half),
        [shape((rows, sources), BF16)],
        [ids],
        [base, weight_turned, *blocks],
        [pltpu.VMEM((sources, levels * touched), BF16)],
    )[0]
    solution_rows = call(
        assemble, [shape((levels, sep_rows, 2 * share))], [ids], [answer, passed]
    )[0]
    return final[None], solution_rows[None]


def solution(mesh):
    in_specs = (
        P("leaf", "col", None),
        P("leaf", None, "col"),
        P("leaf", None, None, "col"),
        P("leaf", None),
        P("leaf", None),
        P("leaf", None, None, None),
        P("leaf", None, None, None),
        P("leaf", None, None, None),
    )
    out_specs = (P("leaf", "col", None), P("leaf", None, None, "col"))
    return jax.shard_map(
        on_device, mesh=mesh, in_specs=in_specs, out_specs=out_specs, check_vma=False
    )
```

```python
import functools

import jax
import jax.numpy as jnp
from jax import lax
from jax.experimental import pallas as pl
from jax.experimental.pallas import tpu as pltpu
from jax.sharding import PartitionSpec as P

F32 = jnp.float32
BF16 = jnp.bfloat16
HIGHEST = lax.Precision.HIGHEST
NN = (((1,), (0,)), ((), ()))
NT = (((1,), (1,)), ((), ()))
TN = (((0,), (0,)), ((), ()))
AXES = ("leaf", "col")


def moved(block, leaf_flip, col_flip):
    leaves, groups = lax.axis_size("leaf"), lax.axis_size("col")
    route = [
        (leaf * groups + col, (leaf ^ leaf_flip) * groups + (col ^ col_flip))
        for leaf in range(leaves)
        for col in range(groups)
    ]
    return lax.ppermute(block, AXES, route)


COST = {}


def call(body, outs, smem, vmem, scratch=(), limit=24):
    title = getattr(body, "func", body).__name__
    cost = None
    if COST.get(title, 1):
        cost = pl.CostEstimate(flops=10**9, bytes_accessed=0, transcendentals=0)
    specs = [pl.BlockSpec(memory_space=pltpu.SMEM)] * len(smem)
    specs += [pl.BlockSpec(memory_space=pltpu.VMEM)] * len(vmem)
    return pl.pallas_call(
        body,
        out_shape=outs,
        in_specs=specs,
        out_specs=[pl.BlockSpec(memory_space=pltpu.VMEM)] * len(outs),
        scratch_shapes=scratch,
        compiler_params=pltpu.CompilerParams(vmem_limit_bytes=limit << 20),
        cost_estimate=pl.CostEstimate(flops=5 * 10**9, bytes_accessed=0, transcendentals=0),
        name=title,
    )(*smem, *vmem)


def dot(a, b, dims):
    return lax.dot_general(a, b, dims, preferred_element_type=F32)


def split(value):
    high = value.astype(BF16)
    return high, (value - high.astype(F32)).astype(BF16)


def dot_split(value, high, low, dims):
    first, second = split(value)
    return dot(first, high, dims) + (dot(first, low, dims) + dot(second, high, dims))


def rows_at(start, size):
    return pl.ds(pl.multiple_of(start, size), size)


def prepare(ids, inverse, link, rhs, q_high, q_low, k_high, k_low, right):
    column, side = ids[0], ids[1]
    levels, share, _ = right.shape
    wide = 2 * share
    for k in range(levels):
        block = inverse[k]
        high, low = split(
            lax.dot_general(block, block, TN, precision=HIGHEST, preferred_element_type=F32)
        )
        q_high[k] = high
        q_low[k] = low
        if k + 1 < levels:
            high, low = split(
                lax.dot_general(link[k], block, NN, precision=HIGHEST, preferred_element_type=F32)
            )
            k_high[k] = high
            k_low[k] = low
        part = rhs[k, :, rows_at(column * wide, wide)].T
        right[k] = jnp.where(side == 0, part[:share], part[share:])


def leaf_products(ids, inverse, rhs, keep, *refs):
    *sends, order = refs
    column = ids[0]
    groups, wide, rows = inverse.shape[0] // rhs.shape[0], keep.shape[1] // 2, rhs.shape[0]
    half = groups // 2
    order[...] = rhs[...].T
    turned = jnp.concatenate(
        [
            order[rows_at((((column ^ j) & (half - 1)) + top * half) * wide, wide), :]
            for j in range(half)
            for top in range(2)
        ],
        axis=0,
    )
    for block in range(groups):
        value = dot(turned, inverse[block * rows : (block + 1) * rows, :], NT)
        keep[block] = value[: 2 * wide]
        for j in range(1, half):
            part = value[2 * wide * j : 2 * wide * (j + 1)]
            sends[(j - 1) * groups + block][...] = part.astype(BF16)


def own_partials(masks, ids, keep, *refs):
    panels, received = refs[: len(masks)], refs[len(masks) : -5]
    mine, low, high, high_own, out = refs[-5:]
    column = ids[0]
    half = low.shape[0]
    for block in range(2 * half):
        value = keep[block]
        for r in received[block :: 2 * half]:
            value += r[...].astype(F32)
        mine[block] = value.astype(BF16)
        if block < half:
            low[block] = value.astype(BF16)
        else:
            high[block - half] = value.astype(BF16)
            high_own[block - half] = value
    total = None
    for mask, panel in zip(masks, panels):
        value = dot(mine[column ^ mask], panel[...], NT)
        total = value if total is None else total + value
    out[...] = total


def partials(masks, ids, mine, early, *refs):
    panels = refs[: len(masks)]
    own, same, other, cross, scratch = refs[len(masks) :]
    column, side, top = ids[0], ids[1], ids[2]
    share = own.shape[0]
    total = early[...]
    for mask, panel in zip(masks, panels):
        total += dot(mine[column ^ mask], panel[...], NT)
    scratch[...] = total

    def piece(which_top, which_side):
        return scratch[rows_at((which_top * 2 + which_side) * share, share), :]

    own[...] = piece(top, side)
    same[...] = piece(1 - top, side).astype(BF16)
    other[...] = piece(top, 1 - side).astype(BF16)
    cross[...] = piece(1 - top, 1 - side).astype(BF16)


def upward(touched, ids, spots, own, same, other, cross, right, k_high, k_low, kept, *sends):
    levels, share, sep_rows = right.shape
    mine = own[...] + same[...].astype(F32)
    theirs = other[...].astype(F32) + cross[...].astype(F32)
    blank = jnp.zeros((share, sep_rows - touched), F32)

    def placed(value, row, k):
        block = value[:, k * touched : (k + 1) * touched] * spots[row + 1, k].astype(F32)
        return pltpu.roll(jnp.concatenate([block, blank], axis=1), spots[row, k], 1)

    carried = None
    for k in range(levels):
        value = placed(mine, 0, k) + placed(theirs, 2, k)
        if k > 0:
            value += carried
        kept[k] = value
        for j in range(min(k, len(sends))):
            sends[j][k - 1 - j] = value.astype(BF16)
        if k + 1 < levels:
            rest = right[k] * (0.5**k) - value
            carried = dot_split(rest, k_high[k], k_low[k], NT)


def downward(touched, lengths, ids, spots, kept, right, q_high, q_low, k_high, k_low, *refs):
    received = refs[: len(lengths)]
    solution, passed, mine, theirs = refs[len(lengths) :]
    levels, _, sep_rows = right.shape
    parent = None
    for k in reversed(range(levels)):
        value = right[k] - kept[k]
        for length, block in zip(lengths, received):
            if length <= k:
                value -= block[k - length].astype(F32)
        answer = dot_split(value, q_high[k], q_low[k], NN)
        if parent is not None:
            answer -= dot_split(parent, k_high[k], k_low[k], NN)
        parent = answer
        solution[k] = answer
        passed[k] = answer
        rounded = answer.astype(BF16).astype(F32)
        for row, out in ((0, mine), (2, theirs)):
            shift = (sep_rows - spots[row, k]) % sep_rows
            piece = pltpu.roll(rounded, shift, 1)[:, :touched] * spots[row + 1, k].astype(F32)
            out[:, k * touched : (k + 1) * touched] = piece.astype(BF16)


def leaf_transposed(masks, half, ids, inverse, *refs):
    panels, blocks = refs[: len(masks)], refs[len(masks) : -2]
    out, weight_turned = refs[-2:]
    column = ids[0]
    rows = inverse.shape[1]
    weight = None
    for mask, panel in zip(masks, panels):
        value = dot(panel[...], inverse[rows_at((column ^ mask) * rows, rows), :], NN)
        weight = value if weight is None else weight + value
    weight_turned[...] = weight.T.astype(BF16)
    total = None
    for block in range(2 * half):
        left = jnp.concatenate(
            [blocks[2 * j + block // half][block % half] for j in range(half)], axis=0
        )
        value = dot(left, inverse[block * rows : (block + 1) * rows, :], NN)
        total = value if total is None else total + value
    wide = total.shape[0] // (2 * half)
    for j in range(half):
        for top in range(2):
            source = ((column ^ j) & (half - 1)) + top * half
            at = (2 * j + top) * wide
            out[:, rows_at(source * wide, wide)] = total[at : at + wide].T


def finish(half, ids, base, weight_turned, *refs):
    out, gathered = refs[-2:]
    blocks = refs[:-2]
    column, side, top = ids[0], ids[1], ids[2]
    share = blocks[0].shape[0]
    for j in range(half):
        inner = (column ^ j) & (half - 1)
        for n, (flip_side, flip_top) in enumerate(((0, 0), (0, 1), (1, 0), (1, 1))):
            which_top = top ^ flip_top
            which_side = side ^ flip_side
            at = ((which_top * half + inner) * 2 + which_side) * share
            gathered[rows_at(at, share), :] = blocks[4 * j + n][...]
    out[...] = (base[...] - dot(weight_turned[...], gathered[...], NT)).astype(BF16)


def assemble(ids, mine, theirs, out):
    side = ids[1]
    for k in range(mine.shape[0]):
        first = jnp.where(side == 0, mine[k], theirs[k])
        second = jnp.where(side == 0, theirs[k], mine[k])
        out[k] = jnp.concatenate([first, second], axis=0).T


def on_device(leaf_rhs, leaf_inverse, panels, pattern, offsets, sep_inverse, sep_link, sep_rhs):
    rhs, inverse = leaf_rhs[0], leaf_inverse[0]
    rows, sources = rhs.shape
    leaves, groups = lax.axis_size("leaf"), lax.axis_size("col")
    levels = leaves.bit_length() - 1
    half = groups // 2
    touched, sep_rows = panels.shape[2], sep_inverse.shape[2]
    share = sources // groups // 2
    panel = panels[0].reshape(levels * touched, rows)
    column = lax.axis_index("col")
    side = lax.axis_index("leaf") & 1
    ids = jnp.stack([column, side, column // half]).astype(jnp.int32)

    def shape(dims, dtype=F32):
        return jax.ShapeDtypeStruct(dims, dtype)

    held = {0: panel, half: moved(panel, 0, half)}
    for mask in range(1, half):
        held[mask] = moved(panel, 0, mask)
    spots = jnp.concatenate([offsets, pattern], axis=0)
    spots = jnp.concatenate([spots, moved(spots, 1, 0)], axis=0)

    mine_rows = (groups, sources // half, rows)
    upper_rows = (half, sources // half, rows)
    keep, *sends = call(
        leaf_products,
        [shape(mine_rows)] + [shape(mine_rows[1:], BF16)] * ((half - 1) * groups),
        [ids],
        [inverse, rhs],
        [pltpu.VMEM((sources, rows), BF16)],
    )
    received = [moved(block, 0, n // groups + 1) for n, block in enumerate(sends)]

    near, far = list(range(half)), list(range(half, groups))
    partial_shape = (sources // half, levels * touched)
    keep, held[half] = lax.optimization_barrier((keep, held[half]))
    mine, low, high, high_own, early = call(
        functools.partial(own_partials, near),
        [shape(mine_rows, BF16)]
        + [shape(upper_rows, BF16)] * 2
        + [shape(upper_rows), shape(partial_shape)],
        [ids],
        [keep] + [held[mask] for mask in near] + received,
    )
    for mask in range(1, half):
        held[half | mask] = moved(held[half], 0, mask)
    piece = (share, levels * touched)
    own, same, other, cross = call(
        functools.partial(partials, far),
        [shape(piece)] + [shape(piece, BF16)] * 3,
        [ids],
        [mine, early] + [held[mask] for mask in far],
        [pltpu.VMEM(partial_shape, F32)],
    )
    high, own, inverses = lax.optimization_barrier((high, own, sep_inverse[0]))
    same, other, cross = moved(same, 0, half), moved(other, 1, 0), moved(cross, 1, half)

    high = moved(high, 0, half)

    q_high, q_low, k_high, k_low, right = call(
        prepare,
        [shape((levels, sep_rows, sep_rows), BF16)] * 2
        + [shape((levels - 1, sep_rows, sep_rows), BF16)] * 2
        + [shape((levels, share, sep_rows))],
        [ids],
        [inverses, sep_link[0], sep_rhs[0]],
    )
    kept, *up_sends = call(
        functools.partial(upward, touched),
        [shape((levels, share, sep_rows))]
        + [shape((levels - length, share, sep_rows), BF16) for length in range(1, levels)],
        [ids, spots],
        [own, same, other, cross, right, k_high, k_low],
    )
    lengths, up_received = [], []
    for delta in range(1, leaves // 2):
        lengths.append(delta.bit_length())
        up_received.append(moved(up_sends[delta.bit_length() - 1], 2 * delta, 0))
    high, *up_received = lax.optimization_barrier((high, *up_received))
    solved_high = (high_own + high.astype(F32)).astype(BF16)
    solved = [low, solved_high]
    for j in range(1, half):
        solved += [moved(low, 0, j), moved(solved_high, 0, j)]
    masks = near + far
    base, weight_turned = call(
        functools.partial(leaf_transposed, masks, half),
        [shape((rows, sources)), shape((rows, levels * touched), BF16)],
        [ids],
        [inverse] + [held[mask] for mask in masks] + solved,
    )

    answer, passed, mine, theirs = call(
        functools.partial(downward, touched, lengths),
        [shape((levels, share, sep_rows))] * 2 + [shape(piece, BF16)] * 2,
        [ids, spots],
        [kept, right, q_high, q_low, k_high, k_low, *up_received],
    )

    blocks = [mine, moved(mine, 0, half), moved(theirs, 1, 0), moved(theirs, 1, half)]
    passed = moved(passed, 1, 0)
    *blocks, base = lax.optimization_barrier((*blocks, base))
    for j in range(1, half):
        blocks += [moved(block, 0, j) for block in blocks[:4]]
    final = call(
        functools.partial(finish, half),
        [shape((rows, sources), BF16)],
        [ids],
        [base, weight_turned, *blocks],
        [pltpu.VMEM((sources, levels * touched), BF16)],
    )[0]
    solution_rows = call(
        assemble, [shape((levels, sep_rows, 2 * share))], [ids], [answer, passed]
    )[0]
    return final[None], solution_rows[None]


def solution(mesh):
    in_specs = (
        P("leaf", "col", None),
        P("leaf", None, "col"),
        P("leaf", None, None, "col"),
        P("leaf", None),
        P("leaf", None),
        P("leaf", None, None, None),
        P("leaf", None, None, None),
        P("leaf", None, None, None),
    )
    out_specs = (P("leaf", "col", None), P("leaf", None, None, "col"))
    return jax.shard_map(
        on_device, mesh=mesh, in_specs=in_specs, out_specs=out_specs, check_vma=False
    )
```

```python
import functools

import jax
import jax.numpy as jnp
from jax import lax
from jax.experimental import pallas as pl
from jax.experimental.pallas import tpu as pltpu
from jax.sharding import PartitionSpec as P

F32 = jnp.float32
BF16 = jnp.bfloat16
HIGHEST = lax.Precision.HIGHEST
NN = (((1,), (0,)), ((), ()))
NT = (((1,), (1,)), ((), ()))
TN = (((0,), (0,)), ((), ()))
AXES = ("leaf", "col")


def moved(block, leaf_flip, col_flip):
    leaves, groups = lax.axis_size("leaf"), lax.axis_size("col")
    route = [
        (leaf * groups + col, (leaf ^ leaf_flip) * groups + (col ^ col_flip))
        for leaf in range(leaves)
        for col in range(groups)
    ]
    return lax.ppermute(block, AXES, route)


COST = {}


def call(body, outs, smem, vmem, scratch=(), limit=24, space=pltpu.VMEM):
    title = getattr(body, "func", body).__name__
    cost = None
    if COST.get(title, 1):
        cost = pl.CostEstimate(flops=10**9, bytes_accessed=0, transcendentals=0)
    specs = [pl.BlockSpec(memory_space=pltpu.SMEM)] * len(smem)
    specs += [pl.BlockSpec(memory_space=pltpu.VMEM)] * len(vmem)
    return pl.pallas_call(
        body,
        out_shape=outs,
        in_specs=specs,
        out_specs=[pl.BlockSpec(memory_space=space)] * len(outs),
        scratch_shapes=scratch,
        compiler_params=pltpu.CompilerParams(vmem_limit_bytes=limit << 20),
        cost_estimate=pl.CostEstimate(flops=5 * 10**9, bytes_accessed=0, transcendentals=0),
        name=title,
    )(*smem, *vmem)


def position():
    column = lax.axis_index("col")
    return column, lax.axis_index("leaf") & 1, column // (lax.axis_size("col") // 2)


def dot(a, b, dims):
    return lax.dot_general(a, b, dims, preferred_element_type=F32)


def split(value):
    high = value.astype(BF16)
    return high, (value - high.astype(F32)).astype(BF16)


def dot_split(value, high, low, dims):
    first, second = split(value)
    return dot(first, high, dims) + (dot(first, low, dims) + dot(second, high, dims))


def rows_at(start, size):
    return pl.ds(pl.multiple_of(start, size), size)


def prepare(spots, inverse, link, rhs, k_high, k_low, right, place):
    column, side, _ = position()
    levels, share, sep_rows = right.shape
    touched = place.shape[1] // 2
    wide = 2 * share
    shift = lax.broadcasted_iota(jnp.int32, (touched, sep_rows), 1) - lax.broadcasted_iota(
        jnp.int32, (touched, sep_rows), 0
    )
    for k in range(levels):
        for n in range(2):
            chosen = jnp.where(shift == spots[2 * n, k], spots[2 * n + 1, k].astype(F32), 0.0)
            place[k, n * touched : (n + 1) * touched] = chosen.astype(BF16)
        if k + 1 < levels:
            high, low = split(
                lax.dot_general(
                    link[k], inverse[k], NN, precision=HIGHEST, preferred_element_type=F32
                )
            )
            k_high[k] = high
            k_low[k] = low
        part = rhs[k, :, rows_at(column * wide, wide)].T
        right[k] = jnp.where(side == 0, part[:share], part[share:])


def squares(inverse, q_high, q_low):
    for k in range(inverse.shape[0]):
        block = inverse[k]
        high, low = split(
            lax.dot_general(block, block, TN, precision=HIGHEST, preferred_element_type=F32)
        )
        q_high[k] = high
        q_low[k] = low


def leaf_products(inverse, rhs, keep, *refs):
    *sends, order = refs
    column, _, _ = position()
    groups, wide, rows = inverse.shape[0] // rhs.shape[0], keep.shape[1] // 2, rhs.shape[0]
    half = groups // 2
    order[...] = rhs[...].T
    turned = jnp.concatenate(
        [
            order[rows_at((((column ^ j) & (half - 1)) + top * half) * wide, wide), :]
            for j in range(half)
            for top in range(2)
        ],
        axis=0,
    )
    for block in range(groups):
        value = dot(turned, inverse[block * rows : (block + 1) * rows, :], NT)
        keep[block] = value[: 2 * wide]
        for j in range(1, half):
            part = value[2 * wide * j : 2 * wide * (j + 1)]
            sends[(j - 1) * groups + block][...] = part.astype(BF16)


def own_partials(masks, keep, *refs):
    panels, received = refs[: len(masks)], refs[len(masks) : -3]
    low, high, out = refs[-3:]
    column, _, top = position()
    half = low.shape[0]
    for block in range(2 * half):
        value = keep[block]
        for r in received[block :: 2 * half]:
            value += r[...].astype(F32)
        if block < half:
            low[block] = value.astype(BF16)
        else:
            high[block - half] = value.astype(BF16)
    out[...] = panel_products(top, column, masks, panels, low, high)


def panel_products(top, column, masks, panels, low, high):
    half = low.shape[0]
    total = None
    for mask, panel in zip(masks, panels):
        block = (column ^ mask) & (half - 1)
        value = dot(jnp.where(top == 0, low[block], high[block]), panel[...], NT)
        total = value if total is None else total + value
    return total


def partials(masks, low, high, early, *refs):
    panels = refs[: len(masks)]
    own, same, other, cross, scratch = refs[len(masks) :]
    column, side, top = position()
    share = own.shape[0]
    scratch[...] = early[...] + panel_products(1 - top, column, masks, panels, low, high)

    def piece(which_top, which_side):
        return scratch[rows_at((which_top * 2 + which_side) * share, share), :]

    own[...] = piece(top, side)
    same[...] = piece(1 - top, side).astype(BF16)
    other[...] = piece(top, 1 - side).astype(BF16)
    cross[...] = piece(1 - top, 1 - side).astype(BF16)


def upward(own, cross, same, other, right, k_high, k_low, place, kept, *sends):
    levels = right.shape[0]
    touched = place.shape[1] // 2
    mine = own[...] + same[...].astype(F32)
    theirs = other[...].astype(F32) + cross[...].astype(F32)
    carried = None
    for k in range(levels):
        at = slice(k * touched, (k + 1) * touched)
        high, low = split(jnp.concatenate([mine[:, at], theirs[:, at]], axis=1))
        value = dot(high, place[k], NN) + dot(low, place[k], NN)
        if k > 0:
            value += carried
        kept[k] = value
        for j in range(min(k, len(sends))):
            sends[j][k - 1 - j] = value.astype(BF16)
        if k + 1 < levels:
            rest = right[k] * (0.5**k) - value
            carried = dot_split(rest, k_high[k], k_low[k], NT)


def downward(lengths, kept, right, q_high, q_low, k_high, k_low, place, *refs):
    received = refs[: len(lengths)]
    solution, mine, theirs, passed = refs[len(lengths) :]
    levels = right.shape[0]
    touched = place.shape[1] // 2
    parent = None
    for k in reversed(range(levels)):
        value = right[k] - kept[k]
        for length, block in zip(lengths, received):
            if length <= k:
                value -= block[k - length].astype(F32)
        answer = dot_split(value, q_high[k], q_low[k], NN)
        if parent is not None:
            answer -= dot_split(parent, k_high[k], k_low[k], NN)
        parent = answer
        solution[k] = answer
        rounded = answer.astype(BF16)
        pieces = dot(rounded, place[k], NT).astype(BF16)
        at = slice(k * touched, (k + 1) * touched)
        mine[:, at] = pieces[:, :touched]
        theirs[:, at] = pieces[:, touched:]
        passed[k] = rounded


def lower_transposed(masks, half, inverse, *refs):
    panels, blocks = refs[: len(masks)], refs[len(masks) : -2]
    out, weight_turned = refs[-2:]
    column, _, _ = position()
    rows = inverse.shape[1]
    weight = None
    for mask, panel in zip(masks, panels):
        value = dot(panel[...], inverse[rows_at((column ^ mask) * rows, rows), :], NN)
        weight = value if weight is None else weight + value
    weight_turned[...] = weight.T.astype(BF16)
    total = None
    for block in range(half):
        left = jnp.concatenate([piece[block] for piece in blocks], axis=0)
        value = dot(left, inverse[block * rows : (block + 1) * rows, :], NN)
        total = value if total is None else total + value
    out[...] = total


def upper_transposed(half, inverse, lower, *refs):
    blocks, out = refs[:-1], refs[-1]
    column, _, _ = position()
    rows = inverse.shape[1]
    total = lower[...]
    for block in range(half):
        left = jnp.concatenate([piece[block] for piece in blocks], axis=0)
        at = (half + block) * rows
        total += dot(left, inverse[at : at + rows, :], NN)
    wide = total.shape[0] // (2 * half)
    for j in range(half):
        for top in range(2):
            source = ((column ^ j) & (half - 1)) + top * half
            at = (2 * j + top) * wide
            out[:, rows_at(source * wide, wide)] = total[at : at + wide].T


def finish(half, base, weight_turned, *refs):
    out, gathered, staged, sems = refs[-4:]
    blocks = refs[:-4]
    column, side, top = position()
    share = blocks[0].shape[0]
    for j in range(half):
        inner = (column ^ j) & (half - 1)
        for n, (flip_side, flip_top) in enumerate(((0, 0), (0, 1), (1, 0), (1, 1))):
            which_top = top ^ flip_top
            which_side = side ^ flip_side
            at = ((which_top * half + inner) * 2 + which_side) * share
            gathered[rows_at(at, share), :] = blocks[4 * j + n][...]
    pieces = sems.shape[0]
    size = out.shape[1] // pieces
    copies = []
    for n in range(pieces):
        part = pl.ds(n * size, size)
        value = base[:, part] - dot(weight_turned[...], gathered[part, :], NT)
        staged[:, part] = value.astype(BF16)
        copy = pltpu.make_async_copy(staged.at[:, part], out.at[:, part], sems.at[n])
        copy.start()
        copies.append(copy)
    for copy in copies:
        copy.wait()


def assemble(mine, passed, out, staged, sems):
    _, side, _ = position()
    copies = []
    for k in range(mine.shape[0]):
        other = passed[k].astype(F32)
        left = jnp.where(side == 0, mine[k], other)
        right = jnp.where(side == 0, other, mine[k])
        staged[k] = jnp.concatenate([left, right], axis=0).T
        copy = pltpu.make_async_copy(staged.at[k], out.at[k], sems.at[k])
        copy.start()
        copies.append(copy)
    for copy in copies:
        copy.wait()


def on_device(leaf_rhs, leaf_inverse, panels, pattern, offsets, sep_inverse, sep_link, sep_rhs):
    rhs, inverse = leaf_rhs[0], leaf_inverse[0]
    rows, sources = rhs.shape
    leaves, groups = lax.axis_size("leaf"), lax.axis_size("col")
    levels = leaves.bit_length() - 1
    half = groups // 2
    touched, sep_rows = panels.shape[2], sep_inverse.shape[2]
    share = sources // groups // 2
    panel = panels[0].reshape(levels * touched, rows)
    def shape(dims, dtype=F32):
        return jax.ShapeDtypeStruct(dims, dtype)

    held = {0: panel, half: moved(panel, 0, half)}
    for mask in range(1, half):
        held[mask] = moved(panel, 0, mask)

    mine_rows = (groups, sources // half, rows)
    upper_rows = (half, sources // half, rows)
    keep, *sends = call(
        leaf_products,
        [shape(mine_rows)] + [shape(mine_rows[1:], BF16)] * ((half - 1) * groups),
        [],
        [inverse, rhs],
        [pltpu.VMEM((sources, rows), BF16)],
    )
    keep, offsets, pattern = lax.optimization_barrier((keep, offsets, pattern))
    spots = jnp.concatenate([offsets, pattern], axis=0)
    spots = jnp.concatenate([spots, moved(spots, 1, 0)], axis=0)
    received = [moved(block, 0, n // groups + 1) for n, block in enumerate(sends)]

    near, far = list(range(half)), list(range(half, groups))
    partial_shape = (sources // half, levels * touched)
    keep, held[half] = lax.optimization_barrier((keep, held[half]))
    low, high, early = call(
        functools.partial(own_partials, near),
        [shape(upper_rows, BF16)] * 2 + [shape(partial_shape)],
        [],
        [keep] + [held[mask] for mask in near] + received,
    )
    for mask in range(1, half):
        held[half | mask] = moved(held[half], 0, mask)
    piece = (share, levels * touched)
    own, same, other, cross = call(
        functools.partial(partials, far),
        [shape(piece)] + [shape(piece, BF16)] * 3,
        [],
        [low, high, early] + [held[mask] for mask in far],
        [pltpu.VMEM(partial_shape, F32)],
    )
    high, own, inverses = lax.optimization_barrier((high, own, sep_inverse[0]))
    cross = moved(cross, 1, half)
    same, other = moved(same, 0, half), moved(other, 1, 0)

    high = moved(high, 0, half)

    k_high, k_low, right, place = call(
        prepare,
        [shape((levels - 1, sep_rows, sep_rows), BF16)] * 2
        + [shape((levels, share, sep_rows)), shape((levels, 2 * touched, sep_rows), BF16)],
        [spots],
        [inverses, sep_link[0], sep_rhs[0]],
    )
    kept, *up_sends = call(
        upward,
        [shape((levels, share, sep_rows))]
        + [shape((levels - length, share, sep_rows), BF16) for length in range(1, levels)],
        [],
        [own, cross, same, other, right, k_high, k_low, place],
    )
    lengths, up_received = [], []
    for delta in range(1, leaves // 2):
        lengths.append(delta.bit_length())
        up_received.append(moved(up_sends[delta.bit_length() - 1], 2 * delta, 0))
    kept, inverse, inverses = lax.optimization_barrier((kept, inverse, inverses))
    masks = near + far
    lower, weight_turned = call(
        functools.partial(lower_transposed, masks, half),
        [shape((sources, rows)), shape((rows, levels * touched), BF16)],
        [],
        [inverse] + [held[mask] for mask in masks] + [low] + [moved(low, 0, j) for j in range(1, half)],
    )
    lower, inverses = lax.optimization_barrier((lower, inverses))
    q_high, q_low = call(
        squares, [shape((levels, sep_rows, sep_rows), BF16)] * 2, [], [inverses]
    )

    answer, mine, theirs, passed = call(
        functools.partial(downward, lengths),
        [shape((levels, share, sep_rows))]
        + [shape(piece, BF16)] * 2
        + [shape((levels, share, sep_rows), BF16)],
        [],
        [kept, right, q_high, q_low, k_high, k_low, place, *up_received],
    )

    high, mine = lax.optimization_barrier((high, mine))
    solved = keep[half:] + high.astype(F32)
    for n, block in enumerate(received):
        if n % groups >= half:
            solved = solved.at[n % groups - half].add(block.astype(F32))
    solved = solved.astype(BF16)
    solved = [solved] + [moved(solved, 0, j) for j in range(1, half)]
    *solved, passed = lax.optimization_barrier((*solved, passed))
    base = call(
        functools.partial(upper_transposed, half),
        [shape((rows, sources))],
        [],
        [inverse, lower, *solved],
    )[0]

    cross = moved(theirs, 1, half)
    blocks = [mine, moved(mine, 0, half), moved(theirs, 1, 0), cross]
    passed = moved(passed, 1, 0)
    *blocks, base = lax.optimization_barrier((*blocks, base))
    weight_turned, passed = lax.optimization_barrier((weight_turned, passed))
    for j in range(1, half):
        blocks += [moved(block, 0, j) for block in blocks[:4]]
    final = call(
        functools.partial(finish, half),
        [shape((rows, sources), BF16)],
        [],
        [base, weight_turned, *blocks],
        [
            pltpu.VMEM((sources, levels * touched), BF16),
            pltpu.VMEM((rows, sources), BF16),
            pltpu.SemaphoreType.DMA((half,)),
        ],
        space=pl.ANY,
    )[0]
    solution_rows = call(
        assemble,
        [shape((levels, sep_rows, 2 * share))],
        [],
        [answer, passed],
        [pltpu.VMEM((levels, sep_rows, 2 * share), F32), pltpu.SemaphoreType.DMA((levels,))],
        space=pl.ANY,
    )[0]
    return final[None], solution_rows[None]


def solution(mesh):
    in_specs = (
        P("leaf", "col", None),
        P("leaf", None, "col"),
        P("leaf", None, None, "col"),
        P("leaf", None),
        P("leaf", None),
        P("leaf", None, None, None),
        P("leaf", None, None, None),
        P("leaf", None, None, None),
    )
    out_specs = (P("leaf", "col", None), P("leaf", None, None, "col"))
    return jax.shard_map(
        on_device, mesh=mesh, in_specs=in_specs, out_specs=out_specs, check_vma=False
    )
```

```python
import functools

import jax
import jax.numpy as jnp
from jax import lax
from jax.experimental import pallas as pl
from jax.experimental.pallas import tpu as pltpu
from jax.sharding import PartitionSpec as P

F32 = jnp.float32
BF16 = jnp.bfloat16
HIGHEST = lax.Precision.HIGHEST
NN = (((1,), (0,)), ((), ()))
NT = (((1,), (1,)), ((), ()))
TN = (((0,), (0,)), ((), ()))
AXES = ("leaf", "col")


def moved(block, leaf_flip, col_flip):
    leaves, groups = lax.axis_size("leaf"), lax.axis_size("col")
    route = [
        (leaf * groups + col, (leaf ^ leaf_flip) * groups + (col ^ col_flip))
        for leaf in range(leaves)
        for col in range(groups)
    ]
    return lax.ppermute(block, AXES, route)


COST = {}


def call(body, outs, smem, vmem, scratch=(), limit=24, space=pltpu.VMEM):
    title = getattr(body, "func", body).__name__
    cost = None
    if COST.get(title, 1):
        cost = pl.CostEstimate(flops=10**9, bytes_accessed=0, transcendentals=0)
    specs = [pl.BlockSpec(memory_space=pltpu.SMEM)] * len(smem)
    specs += [pl.BlockSpec(memory_space=pltpu.VMEM)] * len(vmem)
    return pl.pallas_call(
        body,
        out_shape=outs,
        in_specs=specs,
        out_specs=[pl.BlockSpec(memory_space=space)] * len(outs),
        scratch_shapes=scratch,
        compiler_params=pltpu.CompilerParams(vmem_limit_bytes=limit << 20),
        cost_estimate=pl.CostEstimate(flops=5 * 10**9, bytes_accessed=0, transcendentals=0),
        name=title,
    )(*smem, *vmem)


def position():
    column = lax.axis_index("col")
    return column, lax.axis_index("leaf") & 1, column // (lax.axis_size("col") // 2)


def dot(a, b, dims):
    return lax.dot_general(a, b, dims, preferred_element_type=F32)


def split(value):
    high = value.astype(BF16)
    return high, (value - high.astype(F32)).astype(BF16)


def dot_split(value, high, low, dims):
    first, second = split(value)
    return dot(first, high, dims) + (dot(first, low, dims) + dot(second, high, dims))


def rows_at(start, size):
    return pl.ds(pl.multiple_of(start, size), size)


def prepare(spots, inverse, link, rhs, k_high, k_low, right, place):
    column, side, _ = position()
    levels, share, sep_rows = right.shape
    touched = place.shape[1] // 2
    wide = 2 * share
    shift = lax.broadcasted_iota(jnp.int32, (touched, sep_rows), 1) - lax.broadcasted_iota(
        jnp.int32, (touched, sep_rows), 0
    )
    for k in range(levels):
        for n in range(2):
            chosen = jnp.where(shift == spots[2 * n, k], spots[2 * n + 1, k].astype(F32), 0.0)
            place[k, n * touched : (n + 1) * touched] = chosen.astype(BF16)
        if k + 1 < levels:
            high, low = split(
                lax.dot_general(
                    link[k], inverse[k], NN, precision=HIGHEST, preferred_element_type=F32
                )
            )
            k_high[k] = high
            k_low[k] = low
        part = rhs[k, :, rows_at(column * wide, wide)].T
        right[k] = jnp.where(side == 0, part[:share], part[share:])


def squares(inverse, q_high, q_low):
    for k in range(inverse.shape[0]):
        block = inverse[k]
        high, low = split(
            lax.dot_general(block, block, TN, precision=HIGHEST, preferred_element_type=F32)
        )
        q_high[k] = high
        q_low[k] = low


def leaf_products(inverse, rhs, keep, *refs):
    *sends, order = refs
    column, _, _ = position()
    groups, wide, rows = inverse.shape[0] // rhs.shape[0], keep.shape[1] // 2, rhs.shape[0]
    half = groups // 2
    order[...] = rhs[...].T
    turned = jnp.concatenate(
        [
            order[rows_at((((column ^ j) & (half - 1)) + top * half) * wide, wide), :]
            for j in range(half)
            for top in range(2)
        ],
        axis=0,
    )
    for block in range(groups):
        value = dot(turned, inverse[block * rows : (block + 1) * rows, :], NT)
        keep[block] = value[: 2 * wide]
        for j in range(1, half):
            part = value[2 * wide * j : 2 * wide * (j + 1)]
            sends[(j - 1) * groups + block][...] = part.astype(BF16)


def own_partials(masks, keep, *refs):
    panels, received = refs[: len(masks)], refs[len(masks) : -4]
    low, high, kept, out = refs[-4:]
    column, _, top = position()
    half = low.shape[0]
    for block in range(2 * half):
        value = keep[block]
        for r in received[block :: 2 * half]:
            value += r[...].astype(F32)
        if block < half:
            low[block] = value.astype(BF16)
        else:
            high[block - half] = value.astype(BF16)
            kept[block - half] = value
    out[...] = panel_products(top, column, masks, panels, low, high)


def panel_products(top, column, masks, panels, low, high):
    half = low.shape[0]
    total = None
    for mask, panel in zip(masks, panels):
        block = (column ^ mask) & (half - 1)
        value = dot(jnp.where(top == 0, low[block], high[block]), panel[...], NT)
        total = value if total is None else total + value
    return total


def partials(masks, low, high, early, *refs):
    panels = refs[: len(masks)]
    own, same, other, cross, scratch = refs[len(masks) :]
    column, side, top = position()
    share = own.shape[0]
    scratch[...] = early[...] + panel_products(1 - top, column, masks, panels, low, high)

    def piece(which_top, which_side):
        return scratch[rows_at((which_top * 2 + which_side) * share, share), :]

    own[...] = piece(top, side)
    same[...] = piece(1 - top, side).astype(BF16)
    other[...] = piece(top, 1 - side).astype(BF16)
    cross[...] = piece(1 - top, 1 - side).astype(BF16)


def upward(own, cross, same, other, right, k_high, k_low, place, kept, *sends):
    levels = right.shape[0]
    touched = place.shape[1] // 2
    mine = own[...] + same[...].astype(F32)
    theirs = other[...].astype(F32) + cross[...].astype(F32)
    carried = None
    for k in range(levels):
        at = slice(k * touched, (k + 1) * touched)
        high, low = split(jnp.concatenate([mine[:, at], theirs[:, at]], axis=1))
        value = dot(high, place[k], NN) + dot(low, place[k], NN)
        if k > 0:
            value += carried
        kept[k] = value
        for j in range(min(k, len(sends))):
            sends[j][k - 1 - j] = value.astype(BF16)
        if k + 1 < levels:
            rest = right[k] * (0.5**k) - value
            carried = dot_split(rest, k_high[k], k_low[k], NT)


def downward(lengths, kept, right, q_high, q_low, k_high, k_low, place, *refs):
    received = refs[: len(lengths)]
    solution, mine, theirs, passed = refs[len(lengths) :]
    levels = right.shape[0]
    touched = place.shape[1] // 2
    parent = None
    for k in reversed(range(levels)):
        value = right[k] - kept[k]
        for length, block in zip(lengths, received):
            if length <= k:
                value -= block[k - length].astype(F32)
        answer = dot_split(value, q_high[k], q_low[k], NN)
        if parent is not None:
            answer -= dot_split(parent, k_high[k], k_low[k], NN)
        parent = answer
        solution[k] = answer
        rounded = answer.astype(BF16)
        pieces = dot(rounded, place[k], NT).astype(BF16)
        at = slice(k * touched, (k + 1) * touched)
        mine[:, at] = pieces[:, :touched]
        theirs[:, at] = pieces[:, touched:]
        passed[k] = rounded


def lower_transposed(masks, half, inverse, *refs):
    panels, blocks = refs[: len(masks)], refs[len(masks) : -2]
    out, weight_turned = refs[-2:]
    column, _, _ = position()
    rows = inverse.shape[1]
    weight = None
    for mask, panel in zip(masks, panels):
        value = dot(panel[...], inverse[rows_at((column ^ mask) * rows, rows), :], NN)
        weight = value if weight is None else weight + value
    weight_turned[...] = weight.T.astype(BF16)
    total = None
    for block in range(half):
        left = jnp.concatenate([piece[block] for piece in blocks], axis=0)
        value = dot(left, inverse[block * rows : (block + 1) * rows, :], NN)
        total = value if total is None else total + value
    out[...] = total


def upper_transposed(half, inverse, lower, *refs):
    blocks, out = refs[:-1], refs[-1]
    column, _, _ = position()
    rows = inverse.shape[1]
    total = lower[...]
    for block in range(half):
        left = jnp.concatenate([piece[block] for piece in blocks], axis=0)
        at = (half + block) * rows
        total += dot(left, inverse[at : at + rows, :], NN)
    wide = total.shape[0] // (2 * half)
    for j in range(half):
        for top in range(2):
            source = ((column ^ j) & (half - 1)) + top * half
            at = (2 * j + top) * wide
            out[:, rows_at(source * wide, wide)] = total[at : at + wide].T


def finish(half, base, weight_turned, *refs):
    out, gathered, staged, sems = refs[-4:]
    blocks = refs[:-4]
    column, side, top = position()
    share = blocks[0].shape[0]
    for j in range(half):
        inner = (column ^ j) & (half - 1)
        for n, (flip_side, flip_top) in enumerate(((0, 0), (0, 1), (1, 0), (1, 1))):
            which_top = top ^ flip_top
            which_side = side ^ flip_side
            at = ((which_top * half + inner) * 2 + which_side) * share
            gathered[rows_at(at, share), :] = blocks[4 * j + n][...]
    pieces = sems.shape[0]
    size = out.shape[1] // pieces
    copies = []
    for n in range(pieces):
        part = pl.ds(n * size, size)
        value = base[:, part] - dot(weight_turned[...], gathered[part, :], NT)
        staged[:, part] = value.astype(BF16)
        copy = pltpu.make_async_copy(staged.at[:, part], out.at[:, part], sems.at[n])
        copy.start()
        copies.append(copy)
    for copy in copies:
        copy.wait()


def assemble(mine, passed, out, staged, sems):
    _, side, _ = position()
    copies = []
    for k in range(mine.shape[0]):
        other = passed[k].astype(F32)
        left = jnp.where(side == 0, mine[k], other)
        right = jnp.where(side == 0, other, mine[k])
        staged[k] = jnp.concatenate([left, right], axis=0).T
        copy = pltpu.make_async_copy(staged.at[k], out.at[k], sems.at[k])
        copy.start()
        copies.append(copy)
    for copy in copies:
        copy.wait()


def on_device(leaf_rhs, leaf_inverse, panels, pattern, offsets, sep_inverse, sep_link, sep_rhs):
    rhs, inverse = leaf_rhs[0], leaf_inverse[0]
    rows, sources = rhs.shape
    leaves, groups = lax.axis_size("leaf"), lax.axis_size("col")
    levels = leaves.bit_length() - 1
    half = groups // 2
    touched, sep_rows = panels.shape[2], sep_inverse.shape[2]
    share = sources // groups // 2
    panel = panels[0].reshape(levels * touched, rows)
    def shape(dims, dtype=F32):
        return jax.ShapeDtypeStruct(dims, dtype)

    held = {0: panel, half: moved(panel, 0, half)}
    for mask in range(1, half):
        held[mask] = moved(panel, 0, mask)

    mine_rows = (groups, sources // half, rows)
    upper_rows = (half, sources // half, rows)
    keep, *sends = call(
        leaf_products,
        [shape(mine_rows)] + [shape(mine_rows[1:], BF16)] * ((half - 1) * groups),
        [],
        [inverse, rhs],
        [pltpu.VMEM((sources, rows), BF16)],
    )
    spots = jnp.concatenate([offsets, pattern], axis=0)
    spots = jnp.concatenate([spots, moved(spots, 1, 0)], axis=0)
    received = [moved(block, 0, n // groups + 1) for n, block in enumerate(sends)]

    near, far = list(range(half)), list(range(half, groups))
    partial_shape = (sources // half, levels * touched)
    keep, held[half] = lax.optimization_barrier((keep, held[half]))
    low, high, upper, early = call(
        functools.partial(own_partials, near),
        [shape(upper_rows, BF16)] * 2 + [shape(upper_rows), shape(partial_shape)],
        [],
        [keep] + [held[mask] for mask in near] + received,
    )
    for mask in range(1, half):
        held[half | mask] = moved(held[half], 0, mask)
    piece = (share, levels * touched)
    own, same, other, cross = call(
        functools.partial(partials, far),
        [shape(piece)] + [shape(piece, BF16)] * 3,
        [],
        [low, high, early] + [held[mask] for mask in far],
        [pltpu.VMEM(partial_shape, F32)],
    )
    high, low, own, inverses = lax.optimization_barrier((high, low, own, sep_inverse[0]))
    cross = moved(cross, 1, half)
    same, other = moved(same, 0, half), moved(other, 1, 0)

    high = moved(high, 0, half)

    k_high, k_low, right, place = call(
        prepare,
        [shape((levels - 1, sep_rows, sep_rows), BF16)] * 2
        + [shape((levels, share, sep_rows)), shape((levels, 2 * touched, sep_rows), BF16)],
        [spots],
        [inverses, sep_link[0], sep_rhs[0]],
    )
    kept, *up_sends = call(
        upward,
        [shape((levels, share, sep_rows))]
        + [shape((levels - length, share, sep_rows), BF16) for length in range(1, levels)],
        [],
        [own, cross, same, other, right, k_high, k_low, place],
    )
    lengths, up_received = [], []
    for delta in range(1, leaves // 2):
        lengths.append(delta.bit_length())
        up_received.append(moved(up_sends[delta.bit_length() - 1], 2 * delta, 0))
    kept, inverse, inverses = lax.optimization_barrier((kept, inverse, inverses))
    masks = near + far
    lower, weight_turned = call(
        functools.partial(lower_transposed, masks, half),
        [shape((sources, rows)), shape((rows, levels * touched), BF16)],
        [],
        [inverse] + [held[mask] for mask in masks] + [low] + [moved(low, 0, j) for j in range(1, half)],
    )
    lower, inverses = lax.optimization_barrier((lower, inverses))
    q_high, q_low = call(
        squares, [shape((levels, sep_rows, sep_rows), BF16)] * 2, [], [inverses]
    )

    answer, mine, theirs, passed = call(
        functools.partial(downward, lengths),
        [shape((levels, share, sep_rows))]
        + [shape(piece, BF16)] * 2
        + [shape((levels, share, sep_rows), BF16)],
        [],
        [kept, right, q_high, q_low, k_high, k_low, place, *up_received],
    )

    high, mine = lax.optimization_barrier((high, mine))
    solved = (upper + high.astype(F32)).astype(BF16)
    solved = [solved] + [moved(solved, 0, j) for j in range(1, half)]
    *solved, passed = lax.optimization_barrier((*solved, passed))
    base = call(
        functools.partial(upper_transposed, half),
        [shape((rows, sources))],
        [],
        [inverse, lower, *solved],
    )[0]

    cross = moved(theirs, 1, half)
    blocks = [mine, moved(mine, 0, half), moved(theirs, 1, 0), cross]
    passed = moved(passed, 1, 0)
    *blocks, base = lax.optimization_barrier((*blocks, base))
    weight_turned, passed = lax.optimization_barrier((weight_turned, passed))
    for j in range(1, half):
        blocks += [moved(block, 0, j) for block in blocks[:4]]
    final = call(
        functools.partial(finish, half),
        [shape((rows, sources), BF16)],
        [],
        [base, weight_turned, *blocks],
        [
            pltpu.VMEM((sources, levels * touched), BF16),
            pltpu.VMEM((rows, sources), BF16),
            pltpu.SemaphoreType.DMA((half,)),
        ],
        space=pl.ANY,
    )[0]
    solution_rows = call(
        assemble,
        [shape((levels, sep_rows, 2 * share))],
        [],
        [answer, passed],
        [pltpu.VMEM((levels, sep_rows, 2 * share), F32), pltpu.SemaphoreType.DMA((levels,))],
        space=pl.ANY,
    )[0]
    return final[None], solution_rows[None]


def solution(mesh):
    in_specs = (
        P("leaf", "col", None),
        P("leaf", None, "col"),
        P("leaf", None, None, "col"),
        P("leaf", None),
        P("leaf", None),
        P("leaf", None, None, None),
        P("leaf", None, None, None),
        P("leaf", None, None, None),
    )
    out_specs = (P("leaf", "col", None), P("leaf", None, None, "col"))
    return jax.shard_map(
        on_device, mesh=mesh, in_specs=in_specs, out_specs=out_specs, check_vma=False
    )
```

```python
import functools

import jax
import jax.numpy as jnp
from jax import lax
from jax.experimental import pallas as pl
from jax.experimental.pallas import tpu as pltpu
from jax.sharding import PartitionSpec as P

F32 = jnp.float32
BF16 = jnp.bfloat16
HIGHEST = lax.Precision.HIGHEST
NN = (((1,), (0,)), ((), ()))
NT = (((1,), (1,)), ((), ()))
TN = (((0,), (0,)), ((), ()))
AXES = ("leaf", "col")


def moved(block, leaf_flip, col_flip):
    leaves, groups = lax.axis_size("leaf"), lax.axis_size("col")
    route = [
        (leaf * groups + col, (leaf ^ leaf_flip) * groups + (col ^ col_flip))
        for leaf in range(leaves)
        for col in range(groups)
    ]
    return lax.ppermute(block, AXES, route)


COST = {}


def call(body, outs, smem, vmem, scratch=(), limit=24, space=pltpu.VMEM):
    title = getattr(body, "func", body).__name__
    cost = None
    if COST.get(title, 1):
        cost = pl.CostEstimate(flops=10**9, bytes_accessed=0, transcendentals=0)
    specs = [pl.BlockSpec(memory_space=pltpu.SMEM)] * len(smem)
    specs += [pl.BlockSpec(memory_space=pltpu.VMEM)] * len(vmem)
    return pl.pallas_call(
        body,
        out_shape=outs,
        in_specs=specs,
        out_specs=[pl.BlockSpec(memory_space=space)] * len(outs),
        scratch_shapes=scratch,
        compiler_params=pltpu.CompilerParams(vmem_limit_bytes=limit << 20),
        cost_estimate=pl.CostEstimate(flops=5 * 10**9, bytes_accessed=0, transcendentals=0),
        name=title,
    )(*smem, *vmem)


def position():
    column = lax.axis_index("col")
    return column, lax.axis_index("leaf") & 1, column // (lax.axis_size("col") // 2)


def dot(a, b, dims):
    return lax.dot_general(a, b, dims, preferred_element_type=F32)


def split(value):
    high = value.astype(BF16)
    return high, (value - high.astype(F32)).astype(BF16)


def dot_split(value, high, low, dims):
    first, second = split(value)
    return dot(first, high, dims) + (dot(first, low, dims) + dot(second, high, dims))


def rows_at(start, size):
    return pl.ds(pl.multiple_of(start, size), size)


def prepare(spots, inverse, link, rhs, k_high, k_low, right, place):
    column, side, _ = position()
    levels, share, sep_rows = right.shape
    touched = place.shape[1] // 2
    wide = 2 * share
    shift = lax.broadcasted_iota(jnp.int32, (touched, sep_rows), 1) - lax.broadcasted_iota(
        jnp.int32, (touched, sep_rows), 0
    )
    for k in range(levels):
        for n in range(2):
            chosen = jnp.where(shift == spots[2 * n, k], spots[2 * n + 1, k].astype(F32), 0.0)
            place[k, n * touched : (n + 1) * touched] = chosen.astype(BF16)
        if k + 1 < levels:
            high, low = split(
                lax.dot_general(
                    link[k], inverse[k], NN, precision=HIGHEST, preferred_element_type=F32
                )
            )
            k_high[k] = high
            k_low[k] = low
        part = rhs[k, :, rows_at(column * wide, wide)].T
        right[k] = jnp.where(side == 0, part[:share], part[share:])


def squares(inverse, q_high, q_low):
    for k in range(inverse.shape[0]):
        block = inverse[k]
        high, low = split(
            lax.dot_general(block, block, TN, precision=HIGHEST, preferred_element_type=F32)
        )
        q_high[k] = high
        q_low[k] = low


def leaf_products(inverse, rhs, keep, *refs):
    *sends, order = refs
    column, _, _ = position()
    groups, wide, rows = inverse.shape[0] // rhs.shape[0], keep.shape[1] // 2, rhs.shape[0]
    half = groups // 2
    order[...] = rhs[...].T
    turned = jnp.concatenate(
        [
            order[rows_at((((column ^ j) & (half - 1)) + top * half) * wide, wide), :]
            for j in range(half)
            for top in range(2)
        ],
        axis=0,
    )
    for block in range(groups):
        value = dot(turned, inverse[block * rows : (block + 1) * rows, :], NT)
        keep[block] = value[: 2 * wide]
        for j in range(1, half):
            part = value[2 * wide * j : 2 * wide * (j + 1)]
            sends[(j - 1) * groups + block][...] = part.astype(BF16)


def own_partials(masks, keep, *refs):
    panels, received = refs[: len(masks)], refs[len(masks) : -4]
    low, high, kept, out = refs[-4:]
    column, _, top = position()
    half = low.shape[0]
    for block in range(2 * half):
        value = keep[block]
        for r in received[block :: 2 * half]:
            value += r[...].astype(F32)
        if block < half:
            low[block] = value.astype(BF16)
        else:
            high[block - half] = value.astype(BF16)
            kept[block - half] = value
    out[...] = panel_products(top, column, masks, panels, low, high)


def panel_products(top, column, masks, panels, low, high):
    half = low.shape[0]
    total = None
    for mask, panel in zip(masks, panels):
        block = (column ^ mask) & (half - 1)
        value = dot(jnp.where(top == 0, low[block], high[block]), panel[...], NT)
        total = value if total is None else total + value
    return total


def partials(masks, low, high, early, *refs):
    panels = refs[: len(masks)]
    own, same, other, cross, scratch = refs[len(masks) :]
    column, side, top = position()
    share = own.shape[0]
    scratch[...] = early[...] + panel_products(1 - top, column, masks, panels, low, high)

    def piece(which_top, which_side):
        return scratch[rows_at((which_top * 2 + which_side) * share, share), :]

    own[...] = piece(top, side)
    same[...] = piece(1 - top, side).astype(BF16)
    other[...] = piece(top, 1 - side).astype(BF16)
    cross[...] = piece(1 - top, 1 - side).astype(BF16)


def upward(own, cross, same, other, right, k_high, k_low, place, kept, *sends):
    levels = right.shape[0]
    touched = place.shape[1] // 2
    mine = own[...] + same[...].astype(F32)
    theirs = other[...].astype(F32) + cross[...].astype(F32)
    carried = None
    for k in range(levels):
        at = slice(k * touched, (k + 1) * touched)
        high, low = split(jnp.concatenate([mine[:, at], theirs[:, at]], axis=1))
        value = dot(high, place[k], NN) + dot(low, place[k], NN)
        if k > 0:
            value += carried
        kept[k] = value
        for j in range(min(k, len(sends))):
            sends[j][k - 1 - j] = value.astype(BF16)
        if k + 1 < levels:
            rest = right[k] * (0.5**k) - value
            carried = dot_split(rest, k_high[k], k_low[k], NT)


def downward(lengths, kept, right, q_high, q_low, k_high, k_low, place, *refs):
    received = refs[: len(lengths)]
    solution, mine, theirs, passed = refs[len(lengths) :]
    levels = right.shape[0]
    touched = place.shape[1] // 2
    parent = None
    for k in reversed(range(levels)):
        value = right[k] - kept[k]
        for length, block in zip(lengths, received):
            if length <= k:
                value -= block[k - length].astype(F32)
        answer = dot_split(value, q_high[k], q_low[k], NN)
        if parent is not None:
            answer -= dot_split(parent, k_high[k], k_low[k], NN)
        parent = answer
        solution[k] = answer
        rounded = answer.astype(BF16)
        pieces = dot(rounded, place[k], NT).astype(BF16)
        at = slice(k * touched, (k + 1) * touched)
        mine[:, at] = pieces[:, :touched]
        theirs[:, at] = pieces[:, touched:]
        passed[k] = rounded


def lower_transposed(masks, half, inverse, *refs):
    panels, blocks = refs[: len(masks)], refs[len(masks) : -2]
    out, weight_turned = refs[-2:]
    column, _, _ = position()
    rows = inverse.shape[1]
    weight = None
    for mask, panel in zip(masks, panels):
        value = dot(panel[...], inverse[rows_at((column ^ mask) * rows, rows), :], NN)
        weight = value if weight is None else weight + value
    weight_turned[...] = weight.T.astype(BF16)
    total = None
    for block in range(half):
        left = jnp.concatenate([piece[block] for piece in blocks], axis=0)
        value = dot(left, inverse[block * rows : (block + 1) * rows, :], NN)
        total = value if total is None else total + value
    out[...] = total


def upper_transposed(half, inverse, lower, *refs):
    blocks, out = refs[:-1], refs[-1]
    column, _, _ = position()
    rows = inverse.shape[1]
    total = lower[...]
    for block in range(half):
        left = jnp.concatenate([piece[block] for piece in blocks], axis=0)
        at = (half + block) * rows
        total += dot(left, inverse[at : at + rows, :], NN)
    wide = total.shape[0] // (2 * half)
    for j in range(half):
        for top in range(2):
            source = ((column ^ j) & (half - 1)) + top * half
            at = (2 * j + top) * wide
            out[:, rows_at(source * wide, wide)] = total[at : at + wide].T


def finish(half, base, weight_turned, *refs):
    out, gathered, staged, sems = refs[-4:]
    blocks = refs[:-4]
    column, side, top = position()
    share = blocks[0].shape[0]
    for j in range(half):
        inner = (column ^ j) & (half - 1)
        for n, (flip_side, flip_top) in enumerate(((0, 0), (0, 1), (1, 0), (1, 1))):
            which_top = top ^ flip_top
            which_side = side ^ flip_side
            at = ((which_top * half + inner) * 2 + which_side) * share
            gathered[rows_at(at, share), :] = blocks[4 * j + n][...]
    pieces = sems.shape[0]
    size = out.shape[1] // pieces
    copies = []
    for n in range(pieces):
        part = pl.ds(n * size, size)
        value = base[:, part] - dot(weight_turned[...], gathered[part, :], NT)
        staged[:, part] = value.astype(BF16)
        copy = pltpu.make_async_copy(staged.at[:, part], out.at[:, part], sems.at[n])
        copy.start()
        copies.append(copy)
    for copy in copies:
        copy.wait()


def assemble(mine, passed, out, staged, sems):
    _, side, _ = position()
    copies = []
    for k in range(mine.shape[0]):
        other = passed[k].astype(F32)
        left = jnp.where(side == 0, mine[k], other)
        right = jnp.where(side == 0, other, mine[k])
        staged[k] = jnp.concatenate([left, right], axis=0).T
        copy = pltpu.make_async_copy(staged.at[k], out.at[k], sems.at[k])
        copy.start()
        copies.append(copy)
    for copy in copies:
        copy.wait()


def on_device(leaf_rhs, leaf_inverse, panels, pattern, offsets, sep_inverse, sep_link, sep_rhs):
    rhs, inverse = leaf_rhs[0], leaf_inverse[0]
    rows, sources = rhs.shape
    leaves, groups = lax.axis_size("leaf"), lax.axis_size("col")
    levels = leaves.bit_length() - 1
    half = groups // 2
    touched, sep_rows = panels.shape[2], sep_inverse.shape[2]
    share = sources // groups // 2
    panel = panels[0].reshape(levels * touched, rows)
    def shape(dims, dtype=F32):
        return jax.ShapeDtypeStruct(dims, dtype)

    held = {0: panel, half: moved(panel, 0, half)}

    mine_rows = (groups, sources // half, rows)
    upper_rows = (half, sources // half, rows)
    keep, *sends = call(
        leaf_products,
        [shape(mine_rows)] + [shape(mine_rows[1:], BF16)] * ((half - 1) * groups),
        [],
        [inverse, rhs],
        [pltpu.VMEM((sources, rows), BF16)],
    )
    keep, offsets, pattern, panel = lax.optimization_barrier((keep, offsets, pattern, panel))
    for mask in range(1, half):
        held[mask] = moved(panel, 0, mask)
    spots = jnp.concatenate([offsets, pattern], axis=0)
    spots = jnp.concatenate([spots, moved(spots, 1, 0)], axis=0)
    received = [moved(block, 0, n // groups + 1) for n, block in enumerate(sends)]

    near, far = list(range(half)), list(range(half, groups))
    partial_shape = (sources // half, levels * touched)
    keep, held[half] = lax.optimization_barrier((keep, held[half]))
    low, high, upper, early = call(
        functools.partial(own_partials, near),
        [shape(upper_rows, BF16)] * 2 + [shape(upper_rows), shape(partial_shape)],
        [],
        [keep] + [held[mask] for mask in near] + received,
    )
    for mask in range(1, half):
        held[half | mask] = moved(held[half], 0, mask)
    piece = (share, levels * touched)
    own, same, other, cross = call(
        functools.partial(partials, far),
        [shape(piece)] + [shape(piece, BF16)] * 3,
        [],
        [low, high, early] + [held[mask] for mask in far],
        [pltpu.VMEM(partial_shape, F32)],
    )
    high, low, own, inverses = lax.optimization_barrier((high, low, own, sep_inverse[0]))
    cross = moved(cross, 1, half)
    same, other = moved(same, 0, half), moved(other, 1, 0)

    high = moved(high, 0, half)

    k_high, k_low, right, place = call(
        prepare,
        [shape((levels - 1, sep_rows, sep_rows), BF16)] * 2
        + [shape((levels, share, sep_rows)), shape((levels, 2 * touched, sep_rows), BF16)],
        [spots],
        [inverses, sep_link[0], sep_rhs[0]],
    )
    kept, *up_sends = call(
        upward,
        [shape((levels, share, sep_rows))]
        + [shape((levels - length, share, sep_rows), BF16) for length in range(1, levels)],
        [],
        [own, cross, same, other, right, k_high, k_low, place],
    )
    lengths, up_received = [], []
    for delta in range(1, leaves // 2):
        lengths.append(delta.bit_length())
        up_received.append(moved(up_sends[delta.bit_length() - 1], 2 * delta, 0))
    kept, inverse, inverses = lax.optimization_barrier((kept, inverse, inverses))
    masks = near + far
    lower, weight_turned = call(
        functools.partial(lower_transposed, masks, half),
        [shape((sources, rows)), shape((rows, levels * touched), BF16)],
        [],
        [inverse] + [held[mask] for mask in masks] + [low] + [moved(low, 0, j) for j in range(1, half)],
    )
    lower, inverses = lax.optimization_barrier((lower, inverses))
    q_high, q_low = call(
        squares, [shape((levels, sep_rows, sep_rows), BF16)] * 2, [], [inverses]
    )

    answer, mine, theirs, passed = call(
        functools.partial(downward, lengths),
        [shape((levels, share, sep_rows))]
        + [shape(piece, BF16)] * 2
        + [shape((levels, share, sep_rows), BF16)],
        [],
        [kept, right, q_high, q_low, k_high, k_low, place, *up_received],
    )

    mine, high = lax.optimization_barrier((mine, high))
    solved = (upper + high.astype(F32)).astype(BF16)
    solved = [solved] + [moved(solved, 0, j) for j in range(1, half)]
    *solved, passed = lax.optimization_barrier((*solved, passed))
    base = call(
        functools.partial(upper_transposed, half),
        [shape((rows, sources))],
        [],
        [inverse, lower, *solved],
    )[0]

    cross = moved(theirs, 1, half)
    blocks = [mine, moved(mine, 0, half), moved(theirs, 1, 0), cross]
    passed = moved(passed, 1, 0)
    *blocks, base = lax.optimization_barrier((*blocks, base))
    weight_turned, passed = lax.optimization_barrier((weight_turned, passed))
    for j in range(1, half):
        blocks += [moved(block, 0, j) for block in blocks[:4]]
    final = call(
        functools.partial(finish, half),
        [shape((rows, sources), BF16)],
        [],
        [base, weight_turned, *blocks],
        [
            pltpu.VMEM((sources, levels * touched), BF16),
            pltpu.VMEM((rows, sources), BF16),
            pltpu.SemaphoreType.DMA((half,)),
        ],
        space=pl.ANY,
    )[0]
    solution_rows = call(
        assemble,
        [shape((levels, sep_rows, 2 * share))],
        [],
        [answer, passed],
        [pltpu.VMEM((levels, sep_rows, 2 * share), F32), pltpu.SemaphoreType.DMA((levels,))],
        space=pl.ANY,
    )[0]
    return final[None], solution_rows[None]


def solution(mesh):
    in_specs = (
        P("leaf", "col", None),
        P("leaf", None, "col"),
        P("leaf", None, None, "col"),
        P("leaf", None),
        P("leaf", None),
        P("leaf", None, None, None),
        P("leaf", None, None, None),
        P("leaf", None, None, None),
    )
    out_specs = (P("leaf", "col", None), P("leaf", None, None, "col"))
    return jax.shard_map(
        on_device, mesh=mesh, in_specs=in_specs, out_specs=out_specs, check_vma=False
    )
```

```python
import functools

import jax
import jax.numpy as jnp
from jax import lax
from jax.experimental import pallas as pl
from jax.experimental.pallas import tpu as pltpu
from jax.sharding import PartitionSpec as P

F32 = jnp.float32
BF16 = jnp.bfloat16
HIGHEST = lax.Precision.HIGHEST
NN = (((1,), (0,)), ((), ()))
NT = (((1,), (1,)), ((), ()))
TN = (((0,), (0,)), ((), ()))
AXES = ("leaf", "col")


def moved(block, leaf_flip, col_flip):
    leaves, groups = lax.axis_size("leaf"), lax.axis_size("col")
    route = [
        (leaf * groups + col, (leaf ^ leaf_flip) * groups + (col ^ col_flip))
        for leaf in range(leaves)
        for col in range(groups)
    ]
    return lax.ppermute(block, AXES, route)


COST = {}


def call(body, outs, smem, vmem, scratch=(), limit=24, space=pltpu.VMEM):
    title = getattr(body, "func", body).__name__
    cost = None
    if COST.get(title, 1):
        cost = pl.CostEstimate(flops=10**9, bytes_accessed=0, transcendentals=0)
    specs = [pl.BlockSpec(memory_space=pltpu.SMEM)] * len(smem)
    specs += [pl.BlockSpec(memory_space=pltpu.VMEM)] * len(vmem)
    return pl.pallas_call(
        body,
        out_shape=outs,
        in_specs=specs,
        out_specs=[pl.BlockSpec(memory_space=space)] * len(outs),
        scratch_shapes=scratch,
        compiler_params=pltpu.CompilerParams(vmem_limit_bytes=limit << 20),
        cost_estimate=pl.CostEstimate(flops=5 * 10**9, bytes_accessed=0, transcendentals=0),
        name=title,
    )(*smem, *vmem)


def position():
    column = lax.axis_index("col")
    return column, lax.axis_index("leaf") & 1, column // (lax.axis_size("col") // 2)


def dot(a, b, dims):
    return lax.dot_general(a, b, dims, preferred_element_type=F32)


def split(value):
    high = value.astype(BF16)
    return high, (value - high.astype(F32)).astype(BF16)


def dot_split(value, high, low, dims):
    first, second = split(value)
    return dot(first, high, dims) + (dot(first, low, dims) + dot(second, high, dims))


def rows_at(start, size):
    return pl.ds(pl.multiple_of(start, size), size)


def prepare(spots, inverse, link, rhs, k_high, k_low, right, place):
    column, side, _ = position()
    levels, share, sep_rows = right.shape
    touched = place.shape[1] // 2
    wide = 2 * share
    shift = lax.broadcasted_iota(jnp.int32, (touched, sep_rows), 1) - lax.broadcasted_iota(
        jnp.int32, (touched, sep_rows), 0
    )
    for k in range(levels):
        for n in range(2):
            chosen = jnp.where(shift == spots[2 * n, k], spots[2 * n + 1, k].astype(F32), 0.0)
            place[k, n * touched : (n + 1) * touched] = chosen.astype(BF16)
        if k + 1 < levels:
            high, low = split(
                lax.dot_general(
                    link[k], inverse[k], NN, precision=HIGHEST, preferred_element_type=F32
                )
            )
            k_high[k] = high
            k_low[k] = low
        part = rhs[k, :, rows_at(column * wide, wide)].T
        right[k] = jnp.where(side == 0, part[:share], part[share:])


def squares(inverse, q_high, q_low):
    for k in range(inverse.shape[0]):
        block = inverse[k]
        high, low = split(
            lax.dot_general(block, block, TN, precision=HIGHEST, preferred_element_type=F32)
        )
        q_high[k] = high
        q_low[k] = low


def leaf_products(inverse, rhs, keep, *refs):
    *sends, order = refs
    column, _, _ = position()
    groups, wide, rows = inverse.shape[0] // rhs.shape[0], keep.shape[1] // 2, rhs.shape[0]
    half = groups // 2
    order[...] = rhs[...].T
    turned = jnp.concatenate(
        [
            order[rows_at((((column ^ j) & (half - 1)) + top * half) * wide, wide), :]
            for j in range(half)
            for top in range(2)
        ],
        axis=0,
    )
    for block in range(groups):
        value = dot(turned, inverse[block * rows : (block + 1) * rows, :], NT)
        keep[block] = value[: 2 * wide]
        for j in range(1, half):
            part = value[2 * wide * j : 2 * wide * (j + 1)]
            sends[(j - 1) * groups + block][...] = part.astype(BF16)


def own_partials(masks, keep, *refs):
    panels, received = refs[: len(masks)], refs[len(masks) : -4]
    low, high, kept, out = refs[-4:]
    column, _, top = position()
    half = low.shape[0]
    for block in range(2 * half):
        value = keep[block]
        for r in received[block :: 2 * half]:
            value += r[...].astype(F32)
        if block < half:
            low[block] = value.astype(BF16)
        else:
            high[block - half] = value.astype(BF16)
            kept[block - half] = value
    out[...] = panel_products(top, column, masks, panels, low, high)


def panel_products(top, column, masks, panels, low, high):
    half = low.shape[0]
    total = None
    for mask, panel in zip(masks, panels):
        block = (column ^ mask) & (half - 1)
        value = dot(jnp.where(top == 0, low[block], high[block]), panel[...], NT)
        total = value if total is None else total + value
    return total


def partials(masks, low, high, early, *refs):
    panels = refs[: len(masks)]
    own, same, other, cross, scratch = refs[len(masks) :]
    column, side, top = position()
    share = own.shape[0]
    scratch[...] = early[...] + panel_products(1 - top, column, masks, panels, low, high)

    def piece(which_top, which_side):
        return scratch[rows_at((which_top * 2 + which_side) * share, share), :]

    own[...] = piece(top, side)
    same[...] = piece(1 - top, side).astype(BF16)
    other[...] = piece(top, 1 - side).astype(BF16)
    cross[...] = piece(1 - top, 1 - side).astype(BF16)


def upward(own, cross, same, other, right, k_high, k_low, place, kept, *sends):
    levels = right.shape[0]
    touched = place.shape[1] // 2
    mine = own[...] + same[...].astype(F32)
    theirs = other[...].astype(F32) + cross[...].astype(F32)
    carried = None
    for k in range(levels):
        at = slice(k * touched, (k + 1) * touched)
        high, low = split(jnp.concatenate([mine[:, at], theirs[:, at]], axis=1))
        value = dot(high, place[k], NN) + dot(low, place[k], NN)
        if k > 0:
            value += carried
        kept[k] = value
        for j in range(min(k, len(sends))):
            sends[j][k - 1 - j] = value.astype(BF16)
        if k + 1 < levels:
            rest = right[k] * (0.5**k) - value
            carried = dot_split(rest, k_high[k], k_low[k], NT)


def downward(lengths, kept, right, q_high, q_low, k_high, k_low, place, *refs):
    received = refs[: len(lengths)]
    solution, mine, theirs, passed = refs[len(lengths) :]
    levels = right.shape[0]
    touched = place.shape[1] // 2
    parent = None
    for k in reversed(range(levels)):
        value = right[k] - kept[k]
        for length, block in zip(lengths, received):
            if length <= k:
                value -= block[k - length].astype(F32)
        answer = dot_split(value, q_high[k], q_low[k], NN)
        if parent is not None:
            answer -= dot_split(parent, k_high[k], k_low[k], NN)
        parent = answer
        solution[k] = answer
        rounded = answer.astype(BF16)
        pieces = dot(rounded, place[k], NT).astype(BF16)
        at = slice(k * touched, (k + 1) * touched)
        mine[:, at] = pieces[:, :touched]
        theirs[:, at] = pieces[:, touched:]
        passed[k] = rounded


def lower_transposed(masks, half, inverse, *refs):
    panels, blocks = refs[: len(masks)], refs[len(masks) : -2]
    out, weight_turned = refs[-2:]
    column, _, _ = position()
    rows = inverse.shape[1]
    weight = None
    for mask, panel in zip(masks, panels):
        value = dot(panel[...], inverse[rows_at((column ^ mask) * rows, rows), :], NN)
        weight = value if weight is None else weight + value
    weight_turned[...] = weight.T.astype(BF16)
    total = None
    for block in range(half):
        left = jnp.concatenate([piece[block] for piece in blocks], axis=0)
        value = dot(left, inverse[block * rows : (block + 1) * rows, :], NN)
        total = value if total is None else total + value
    out[...] = total


def upper_transposed(half, inverse, lower, *refs):
    blocks, out = refs[:-1], refs[-1]
    column, _, _ = position()
    rows = inverse.shape[1]
    total = lower[...]
    for block in range(half):
        left = jnp.concatenate([piece[block] for piece in blocks], axis=0)
        at = (half + block) * rows
        total += dot(left, inverse[at : at + rows, :], NN)
    wide = total.shape[0] // (2 * half)
    for j in range(half):
        for top in range(2):
            source = ((column ^ j) & (half - 1)) + top * half
            at = (2 * j + top) * wide
            out[:, rows_at(source * wide, wide)] = total[at : at + wide].T


def finish(half, base, weight_turned, *refs):
    out, gathered, staged, sems = refs[-4:]
    blocks = refs[:-4]
    column, side, top = position()
    share = blocks[0].shape[0]
    for j in range(half):
        inner = (column ^ j) & (half - 1)
        for n, (flip_side, flip_top) in enumerate(((0, 0), (0, 1), (1, 0), (1, 1))):
            which_top = top ^ flip_top
            which_side = side ^ flip_side
            at = ((which_top * half + inner) * 2 + which_side) * share
            gathered[rows_at(at, share), :] = blocks[4 * j + n][...]
    pieces = sems.shape[0]
    size = out.shape[1] // pieces
    copies = []
    for n in range(pieces):
        part = pl.ds(n * size, size)
        value = base[:, part] - dot(weight_turned[...], gathered[part, :], NT)
        staged[:, part] = value.astype(BF16)
        copy = pltpu.make_async_copy(staged.at[:, part], out.at[:, part], sems.at[n])
        copy.start()
        copies.append(copy)
    for copy in copies:
        copy.wait()


def assemble(mine, passed, out, staged, sems):
    _, side, _ = position()
    copies = []
    for k in range(mine.shape[0]):
        other = passed[k].astype(F32)
        left = jnp.where(side == 0, mine[k], other)
        right = jnp.where(side == 0, other, mine[k])
        staged[k] = jnp.concatenate([left, right], axis=0).T
        copy = pltpu.make_async_copy(staged.at[k], out.at[k], sems.at[k])
        copy.start()
        copies.append(copy)
    for copy in copies:
        copy.wait()


def on_device(leaf_rhs, leaf_inverse, panels, pattern, offsets, sep_inverse, sep_link, sep_rhs):
    rhs, inverse = leaf_rhs[0], leaf_inverse[0]
    rows, sources = rhs.shape
    leaves, groups = lax.axis_size("leaf"), lax.axis_size("col")
    levels = leaves.bit_length() - 1
    half = groups // 2
    touched, sep_rows = panels.shape[2], sep_inverse.shape[2]
    share = sources // groups // 2
    panel = panels[0].reshape(levels * touched, rows)
    def shape(dims, dtype=F32):
        return jax.ShapeDtypeStruct(dims, dtype)

    held = {0: panel, half: moved(panel, 0, half)}
    for mask in range(1, half):
        held[mask] = moved(panel, 0, mask)

    mine_rows = (groups, sources // half, rows)
    upper_rows = (half, sources // half, rows)
    keep, *sends = call(
        leaf_products,
        [shape(mine_rows)] + [shape(mine_rows[1:], BF16)] * ((half - 1) * groups),
        [],
        [inverse, rhs],
        [pltpu.VMEM((sources, rows), BF16)],
    )
    spots = jnp.concatenate([offsets, pattern], axis=0)
    spots = jnp.concatenate([spots, moved(spots, 1, 0)], axis=0)
    received = [moved(block, 0, n // groups + 1) for n, block in enumerate(sends)]

    near, far = list(range(half)), list(range(half, groups))
    partial_shape = (sources // half, levels * touched)
    keep, held[half] = lax.optimization_barrier((keep, held[half]))
    low, high, upper, early = call(
        functools.partial(own_partials, near),
        [shape(upper_rows, BF16)] * 2 + [shape(upper_rows), shape(partial_shape)],
        [],
        [keep] + [held[mask] for mask in near] + received,
    )
    for mask in range(1, half):
        held[half | mask] = moved(held[half], 0, mask)
    piece = (share, levels * touched)
    own, same, other, cross = call(
        functools.partial(partials, far),
        [shape(piece)] + [shape(piece, BF16)] * 3,
        [],
        [low, high, early] + [held[mask] for mask in far],
        [pltpu.VMEM(partial_shape, F32)],
    )
    high, low, own, inverses, spots = lax.optimization_barrier((high, low, own, sep_inverse[0], spots))
    cross = moved(cross, 1, half)
    same, other = moved(same, 0, half), moved(other, 1, 0)

    high = moved(high, 0, half)

    k_high, k_low, right, place = call(
        prepare,
        [shape((levels - 1, sep_rows, sep_rows), BF16)] * 2
        + [shape((levels, share, sep_rows)), shape((levels, 2 * touched, sep_rows), BF16)],
        [spots],
        [inverses, sep_link[0], sep_rhs[0]],
    )
    kept, *up_sends = call(
        upward,
        [shape((levels, share, sep_rows))]
        + [shape((levels - length, share, sep_rows), BF16) for length in range(1, levels)],
        [],
        [own, cross, same, other, right, k_high, k_low, place],
    )
    lengths, up_received = [], []
    for delta in range(1, leaves // 2):
        lengths.append(delta.bit_length())
        up_received.append(moved(up_sends[delta.bit_length() - 1], 2 * delta, 0))
    kept, inverse, inverses = lax.optimization_barrier((kept, inverse, inverses))
    masks = near + far
    lower, weight_turned = call(
        functools.partial(lower_transposed, masks, half),
        [shape((sources, rows)), shape((rows, levels * touched), BF16)],
        [],
        [inverse] + [held[mask] for mask in masks] + [low] + [moved(low, 0, j) for j in range(1, half)],
    )
    lower, inverses = lax.optimization_barrier((lower, inverses))
    q_high, q_low = call(
        squares, [shape((levels, sep_rows, sep_rows), BF16)] * 2, [], [inverses]
    )

    answer, mine, theirs, passed = call(
        functools.partial(downward, lengths),
        [shape((levels, share, sep_rows))]
        + [shape(piece, BF16)] * 2
        + [shape((levels, share, sep_rows), BF16)],
        [],
        [kept, right, q_high, q_low, k_high, k_low, place, *up_received],
    )

    high, mine = lax.optimization_barrier((high, mine))
    solved = (upper + high.astype(F32)).astype(BF16)
    solved = [solved] + [moved(solved, 0, j) for j in range(1, half)]
    *solved, passed = lax.optimization_barrier((*solved, passed))
    base = call(
        functools.partial(upper_transposed, half),
        [shape((rows, sources))],
        [],
        [inverse, lower, *solved],
    )[0]

    cross = moved(theirs, 1, half)
    blocks = [mine, moved(mine, 0, half), moved(theirs, 1, 0), cross]
    passed = moved(passed, 1, 0)
    *blocks, base = lax.optimization_barrier((*blocks, base))
    weight_turned, passed = lax.optimization_barrier((weight_turned, passed))
    for j in range(1, half):
        blocks += [moved(block, 0, j) for block in blocks[:4]]
    final = call(
        functools.partial(finish, half),
        [shape((rows, sources), BF16)],
        [],
        [base, weight_turned, *blocks],
        [
            pltpu.VMEM((sources, levels * touched), BF16),
            pltpu.VMEM((rows, sources), BF16),
            pltpu.SemaphoreType.DMA((groups,)),
        ],
        space=pl.ANY,
    )[0]
    solution_rows = call(
        assemble,
        [shape((levels, sep_rows, 2 * share))],
        [],
        [answer, passed],
        [pltpu.VMEM((levels, sep_rows, 2 * share), F32), pltpu.SemaphoreType.DMA((levels,))],
        space=pl.ANY,
    )[0]
    return final[None], solution_rows[None]


def solution(mesh):
    in_specs = (
        P("leaf", "col", None),
        P("leaf", None, "col"),
        P("leaf", None, None, "col"),
        P("leaf", None),
        P("leaf", None),
        P("leaf", None, None, None),
        P("leaf", None, None, None),
        P("leaf", None, None, None),
    )
    out_specs = (P("leaf", "col", None), P("leaf", None, None, "col"))
    return jax.shard_map(
        on_device, mesh=mesh, in_specs=in_specs, out_specs=out_specs, check_vma=False
    )
```

```python
import functools

import jax
import jax.numpy as jnp
from jax import lax
from jax.experimental import pallas as pl
from jax.experimental.pallas import tpu as pltpu
from jax.sharding import PartitionSpec as P

F32 = jnp.float32
BF16 = jnp.bfloat16
HIGHEST = lax.Precision.HIGHEST
NN = (((1,), (0,)), ((), ()))
NT = (((1,), (1,)), ((), ()))
TN = (((0,), (0,)), ((), ()))
AXES = ("leaf", "col")


def moved(block, leaf_flip, col_flip):
    leaves, groups = lax.axis_size("leaf"), lax.axis_size("col")
    route = [
        (leaf * groups + col, (leaf ^ leaf_flip) * groups + (col ^ col_flip))
        for leaf in range(leaves)
        for col in range(groups)
    ]
    return lax.ppermute(block, AXES, route)


COST = {}


def call(body, outs, smem, vmem, scratch=(), limit=24, space=pltpu.VMEM):
    title = getattr(body, "func", body).__name__
    cost = None
    if COST.get(title, 1):
        cost = pl.CostEstimate(flops=10**9, bytes_accessed=0, transcendentals=0)
    specs = [pl.BlockSpec(memory_space=pltpu.SMEM)] * len(smem)
    specs += [pl.BlockSpec(memory_space=pltpu.VMEM)] * len(vmem)
    return pl.pallas_call(
        body,
        out_shape=outs,
        in_specs=specs,
        out_specs=[pl.BlockSpec(memory_space=space)] * len(outs),
        scratch_shapes=scratch,
        compiler_params=pltpu.CompilerParams(vmem_limit_bytes=limit << 20),
        cost_estimate=pl.CostEstimate(flops=5 * 10**9, bytes_accessed=0, transcendentals=0),
        name=title,
    )(*smem, *vmem)


def position():
    column = lax.axis_index("col")
    return column, lax.axis_index("leaf") & 1, column // (lax.axis_size("col") // 2)


def dot(a, b, dims):
    return lax.dot_general(a, b, dims, preferred_element_type=F32)


def split(value):
    high = value.astype(BF16)
    return high, (value - high.astype(F32)).astype(BF16)


def dot_split(value, high, low, dims):
    first, second = split(value)
    return dot(first, high, dims) + (dot(first, low, dims) + dot(second, high, dims))


def rows_at(start, size):
    return pl.ds(pl.multiple_of(start, size), size)


def prepare(spots, inverse, link, rhs, k_high, k_low, right, place):
    column, side, _ = position()
    levels, share, sep_rows = right.shape
    touched = place.shape[1] // 2
    wide = 2 * share
    shift = lax.broadcasted_iota(jnp.int32, (touched, sep_rows), 1) - lax.broadcasted_iota(
        jnp.int32, (touched, sep_rows), 0
    )
    for k in range(levels):
        for n in range(2):
            chosen = jnp.where(shift == spots[2 * n, k], spots[2 * n + 1, k].astype(F32), 0.0)
            place[k, n * touched : (n + 1) * touched] = chosen.astype(BF16)
        if k + 1 < levels:
            high, low = split(
                lax.dot_general(
                    link[k], inverse[k], NN, precision=HIGHEST, preferred_element_type=F32
                )
            )
            k_high[k] = high
            k_low[k] = low
        part = rhs[k, :, rows_at(column * wide, wide)].T
        right[k] = jnp.where(side == 0, part[:share], part[share:])


def squares(inverse, q_high, q_low):
    for k in range(inverse.shape[0]):
        block = inverse[k]
        high, low = split(
            lax.dot_general(block, block, TN, precision=HIGHEST, preferred_element_type=F32)
        )
        q_high[k] = high
        q_low[k] = low


def leaf_products(inverse, rhs, keep, *refs):
    *sends, order = refs
    column, _, _ = position()
    groups, wide, rows = inverse.shape[0] // rhs.shape[0], keep.shape[1] // 2, rhs.shape[0]
    half = groups // 2
    order[...] = rhs[...].T
    turned = jnp.concatenate(
        [
            order[rows_at((((column ^ j) & (half - 1)) + top * half) * wide, wide), :]
            for j in range(half)
            for top in range(2)
        ],
        axis=0,
    )
    for block in range(groups):
        value = dot(turned, inverse[block * rows : (block + 1) * rows, :], NT)
        keep[block] = value[: 2 * wide]
        for j in range(1, half):
            part = value[2 * wide * j : 2 * wide * (j + 1)]
            sends[(j - 1) * groups + block][...] = part.astype(BF16)


def own_partials(masks, keep, *refs):
    panels, received = refs[: len(masks)], refs[len(masks) : -4]
    low, high, kept, out = refs[-4:]
    column, _, top = position()
    half = low.shape[0]
    for block in range(2 * half):
        value = keep[block]
        for r in received[block :: 2 * half]:
            value += r[...].astype(F32)
        if block < half:
            low[block] = value.astype(BF16)
        else:
            high[block - half] = value.astype(BF16)
            kept[block - half] = value
    out[...] = panel_products(top, column, masks, panels, low, high)


def panel_products(top, column, masks, panels, low, high):
    half = low.shape[0]
    total = None
    for mask, panel in zip(masks, panels):
        block = (column ^ mask) & (half - 1)
        value = dot(jnp.where(top == 0, low[block], high[block]), panel[...], NT)
        total = value if total is None else total + value
    return total


def partials(masks, low, high, early, *refs):
    panels = refs[: len(masks)]
    own, same, other, cross, scratch = refs[len(masks) :]
    column, side, top = position()
    share = own.shape[0]
    scratch[...] = early[...] + panel_products(1 - top, column, masks, panels, low, high)

    def piece(which_top, which_side):
        return scratch[rows_at((which_top * 2 + which_side) * share, share), :]

    own[...] = piece(top, side)
    same[...] = piece(1 - top, side).astype(BF16)
    other[...] = piece(top, 1 - side).astype(BF16)
    cross[...] = piece(1 - top, 1 - side).astype(BF16)


def upward(own, cross, same, other, right, k_high, k_low, place, kept, *sends):
    levels = right.shape[0]
    touched = place.shape[1] // 2
    mine = own[...] + same[...].astype(F32)
    theirs = other[...].astype(F32) + cross[...].astype(F32)
    carried = None
    for k in range(levels):
        at = slice(k * touched, (k + 1) * touched)
        high, low = split(jnp.concatenate([mine[:, at], theirs[:, at]], axis=1))
        value = dot(high, place[k], NN) + dot(low, place[k], NN)
        if k > 0:
            value += carried
        kept[k] = value
        for j in range(min(k, len(sends))):
            sends[j][k - 1 - j] = value.astype(BF16)
        if k + 1 < levels:
            rest = right[k] * (0.5**k) - value
            carried = dot_split(rest, k_high[k], k_low[k], NT)


def downward(lengths, kept, right, q_high, q_low, k_high, k_low, place, *refs):
    received = refs[: len(lengths)]
    solution, mine, theirs, passed = refs[len(lengths) :]
    levels = right.shape[0]
    touched = place.shape[1] // 2
    parent = None
    for k in reversed(range(levels)):
        value = right[k] - kept[k]
        for length, block in zip(lengths, received):
            if length <= k:
                value -= block[k - length].astype(F32)
        answer = dot_split(value, q_high[k], q_low[k], NN)
        if parent is not None:
            answer -= dot_split(parent, k_high[k], k_low[k], NN)
        parent = answer
        solution[k] = answer
        rounded = answer.astype(BF16)
        pieces = dot(rounded, place[k], NT).astype(BF16)
        at = slice(k * touched, (k + 1) * touched)
        mine[:, at] = pieces[:, :touched]
        theirs[:, at] = pieces[:, touched:]
        passed[k] = rounded


def lower_transposed(masks, half, inverse, *refs):
    panels, blocks = refs[: len(masks)], refs[len(masks) : -2]
    out, weight_turned = refs[-2:]
    column, _, _ = position()
    rows = inverse.shape[1]
    weight = None
    for mask, panel in zip(masks, panels):
        value = dot(panel[...], inverse[rows_at((column ^ mask) * rows, rows), :], NN)
        weight = value if weight is None else weight + value
    weight_turned[...] = weight.T.astype(BF16)
    total = None
    for block in range(half):
        left = jnp.concatenate([piece[block] for piece in blocks], axis=0)
        value = dot(left, inverse[block * rows : (block + 1) * rows, :], NN)
        total = value if total is None else total + value
    out[...] = total


def upper_transposed(half, inverse, lower, *refs):
    blocks, out = refs[:-1], refs[-1]
    column, _, _ = position()
    rows = inverse.shape[1]
    total = lower[...]
    for block in range(half):
        left = jnp.concatenate([piece[block] for piece in blocks], axis=0)
        at = (half + block) * rows
        total += dot(left, inverse[at : at + rows, :], NN)
    wide = total.shape[0] // (2 * half)
    for j in range(half):
        for top in range(2):
            source = ((column ^ j) & (half - 1)) + top * half
            at = (2 * j + top) * wide
            out[:, rows_at(source * wide, wide)] = total[at : at + wide].T


def finish(half, base, weight_turned, *refs):
    out, gathered, staged, sems = refs[-4:]
    blocks = refs[:-4]
    column, side, top = position()
    share = blocks[0].shape[0]
    for j in range(half):
        inner = (column ^ j) & (half - 1)
        for n, (flip_side, flip_top) in enumerate(((0, 0), (0, 1), (1, 0), (1, 1))):
            which_top = top ^ flip_top
            which_side = side ^ flip_side
            at = ((which_top * half + inner) * 2 + which_side) * share
            gathered[rows_at(at, share), :] = blocks[4 * j + n][...]
    pieces = sems.shape[0]
    size = out.shape[1] // pieces
    copies = []
    for n in range(pieces):
        part = pl.ds(n * size, size)
        value = base[:, part] - dot(weight_turned[...], gathered[part, :], NT)
        staged[:, part] = value.astype(BF16)
        copy = pltpu.make_async_copy(staged.at[:, part], out.at[:, part], sems.at[n])
        copy.start()
        copies.append(copy)
    for copy in copies:
        copy.wait()


def assemble(mine, passed, out, staged, sems):
    _, side, _ = position()
    copies = []
    for k in range(mine.shape[0]):
        other = passed[k].astype(F32)
        left = jnp.where(side == 0, mine[k], other)
        right = jnp.where(side == 0, other, mine[k])
        staged[k] = jnp.concatenate([left, right], axis=0).T
        copy = pltpu.make_async_copy(staged.at[k], out.at[k], sems.at[k])
        copy.start()
        copies.append(copy)
    for copy in copies:
        copy.wait()


def on_device(leaf_rhs, leaf_inverse, panels, pattern, offsets, sep_inverse, sep_link, sep_rhs):
    rhs, inverse = leaf_rhs[0], leaf_inverse[0]
    rows, sources = rhs.shape
    leaves, groups = lax.axis_size("leaf"), lax.axis_size("col")
    levels = leaves.bit_length() - 1
    half = groups // 2
    touched, sep_rows = panels.shape[2], sep_inverse.shape[2]
    share = sources // groups // 2
    panel = panels[0].reshape(levels * touched, rows)
    def shape(dims, dtype=F32):
        return jax.ShapeDtypeStruct(dims, dtype)

    held = {0: panel, half: moved(panel, 0, half)}

    mine_rows = (groups, sources // half, rows)
    upper_rows = (half, sources // half, rows)
    keep, *sends = call(
        leaf_products,
        [shape(mine_rows)] + [shape(mine_rows[1:], BF16)] * ((half - 1) * groups),
        [],
        [inverse, rhs],
        [pltpu.VMEM((sources, rows), BF16)],
    )
    keep, panel = lax.optimization_barrier((keep, panel))
    for mask in range(1, half):
        held[mask] = moved(panel, 0, mask)
    spots = jnp.concatenate([offsets, pattern], axis=0)
    spots = jnp.concatenate([spots, moved(spots, 1, 0)], axis=0)
    received = [moved(block, 0, n // groups + 1) for n, block in enumerate(sends)]

    near, far = list(range(half)), list(range(half, groups))
    partial_shape = (sources // half, levels * touched)
    keep, held[half] = lax.optimization_barrier((keep, held[half]))
    low, high, upper, early = call(
        functools.partial(own_partials, near),
        [shape(upper_rows, BF16)] * 2 + [shape(upper_rows), shape(partial_shape)],
        [],
        [keep] + [held[mask] for mask in near] + received,
    )
    for mask in range(1, half):
        held[half | mask] = moved(held[half], 0, mask)
    piece = (share, levels * touched)
    own, same, other, cross = call(
        functools.partial(partials, far),
        [shape(piece)] + [shape(piece, BF16)] * 3,
        [],
        [low, high, early] + [held[mask] for mask in far],
        [pltpu.VMEM(partial_shape, F32)],
    )
    high, low, own, inverses = lax.optimization_barrier((high, low, own, sep_inverse[0]))
    cross = moved(cross, 1, half)
    same, other = moved(same, 0, half), moved(other, 1, 0)

    high = moved(high, 0, half)

    k_high, k_low, right, place = call(
        prepare,
        [shape((levels - 1, sep_rows, sep_rows), BF16)] * 2
        + [shape((levels, share, sep_rows)), shape((levels, 2 * touched, sep_rows), BF16)],
        [spots],
        [inverses, sep_link[0], sep_rhs[0]],
    )
    kept, *up_sends = call(
        upward,
        [shape((levels, share, sep_rows))]
        + [shape((levels - length, share, sep_rows), BF16) for length in range(1, levels)],
        [],
        [own, cross, same, other, right, k_high, k_low, place],
    )
    lengths, up_received = [], []
    for delta in range(1, leaves // 2):
        lengths.append(delta.bit_length())
        up_received.append(moved(up_sends[delta.bit_length() - 1], 2 * delta, 0))
    kept, inverse, inverses = lax.optimization_barrier((kept, inverse, inverses))
    masks = near + far
    lower, weight_turned = call(
        functools.partial(lower_transposed, masks, half),
        [shape((sources, rows)), shape((rows, levels * touched), BF16)],
        [],
        [inverse] + [held[mask] for mask in masks] + [low] + [moved(low, 0, j) for j in range(1, half)],
    )
    lower, inverses = lax.optimization_barrier((lower, inverses))
    q_high, q_low = call(
        squares, [shape((levels, sep_rows, sep_rows), BF16)] * 2, [], [inverses]
    )

    answer, mine, theirs, passed = call(
        functools.partial(downward, lengths),
        [shape((levels, share, sep_rows))]
        + [shape(piece, BF16)] * 2
        + [shape((levels, share, sep_rows), BF16)],
        [],
        [kept, right, q_high, q_low, k_high, k_low, place, *up_received],
    )

    mine, high = lax.optimization_barrier((mine, high))
    solved = (upper + high.astype(F32)).astype(BF16)
    solved = [solved] + [moved(solved, 0, j) for j in range(1, half)]
    *solved, passed = lax.optimization_barrier((*solved, passed))
    base = call(
        functools.partial(upper_transposed, half),
        [shape((rows, sources))],
        [],
        [inverse, lower, *solved],
    )[0]

    cross = moved(theirs, 1, half)
    blocks = [mine, moved(mine, 0, half), moved(theirs, 1, 0), cross]
    passed = moved(passed, 1, 0)
    *blocks, base = lax.optimization_barrier((*blocks, base))
    weight_turned, passed = lax.optimization_barrier((weight_turned, passed))
    for j in range(1, half):
        blocks += [moved(block, 0, j) for block in blocks[:4]]
    final = call(
        functools.partial(finish, half),
        [shape((rows, sources), BF16)],
        [],
        [base, weight_turned, *blocks],
        [
            pltpu.VMEM((sources, levels * touched), BF16),
            pltpu.VMEM((rows, sources), BF16),
            pltpu.SemaphoreType.DMA((groups,)),
        ],
        space=pl.ANY,
    )[0]
    solution_rows = call(
        assemble,
        [shape((levels, sep_rows, 2 * share))],
        [],
        [answer, passed],
        [pltpu.VMEM((levels, sep_rows, 2 * share), F32), pltpu.SemaphoreType.DMA((levels,))],
        space=pl.ANY,
    )[0]
    return final[None], solution_rows[None]


def solution(mesh):
    in_specs = (
        P("leaf", "col", None),
        P("leaf", None, "col"),
        P("leaf", None, None, "col"),
        P("leaf", None),
        P("leaf", None),
        P("leaf", None, None, None),
        P("leaf", None, None, None),
        P("leaf", None, None, None),
    )
    out_specs = (P("leaf", "col", None), P("leaf", None, None, "col"))
    return jax.shard_map(
        on_device, mesh=mesh, in_specs=in_specs, out_specs=out_specs, check_vma=False
    )
```
